256 devices in a mesh: tm: 64 (over x, z, core), chan: 4 (over y).
Axes of the slice: x: 4, y: 4, z: 8, core: 2. Of those that a mesh axis runs over, the one named last changes fastest.
Arguments:
- filterbank: bfloat16 [4096, 262144], P(('chan', 'tm')), may hold values from -6 to 6
- channel_mask: int32 [4096], P(('chan', 'tm')), may hold values 0 or 1
- delays: int32 [32, 64], P(None, 'chan'), may hold values from 0 to 127
- readers: int32 [2048, 8, 1], P('tm'), may hold values from 0 to 63; in each aligned block of 256 rows (0 to 255, 256 to 511, ..., all dimensions but the last counted through in order) at most 8 rows name the same one
- stretch: float32 [8], replicated, may hold values from 0.5 to 1.8
Outputs:
- series: bfloat16 [32, 262144], P('chan', 'tm')
- stacked: bfloat16 [8, 32, 8192], P(None, 'chan', 'tm')
The draws below stay inside these ranges and needn't reach their ends.
Inputs may be any that keep to these rules, and one draw needn't show every extreme that they name: `readers`: among the 256 entries of the 32 blocks of one index of tm, no reader appears more than 8 times, and some reader appears exactly 8 times.
All inputs are finite; a program needn't handle non-finite values. No bound on the sum of `channel_mask` on one device may be relied on, other than what follows from the above.
Results may differ from the reference program's by a relative error of at most 0.0068.
Values may be sent and summed in bfloat16 or wider, within the bound.
A program may use at most 64 MiB of HBM per device.

```python
import math
import jax
import jax.numpy as jnp
import numpy as np
from jax import lax

NCH = 4096
SUBCH = 64
NDM = 32
BLK = 128
NACC = 8
NT = 262144
NBD = 32
NB = 2048
NSUB = 64
READERS = 64
CAP = 8
N_TM = 64


def set_ends(drawn, key, low, top_value):
    longest = drawn.shape.index(max(drawn.shape))
    spots = []
    for shift in (0, 1):
        where = [jax.random.randint(jax.random.fold_in(key, axis), (), 0, length) for axis, length in enumerate(drawn.shape)]
        where[longest] = (where[longest] + shift) % drawn.shape[longest]
        spots.append(tuple(where))
    return drawn.at[spots[0]].set(low).at[spots[1]].set(top_value)


def levels(stream_key, extent, pieces, least, high):
    def one(axis_at, shards_of):
        heights = jax.random.uniform(jax.random.fold_in(jax.random.fold_in(stream_key, 6), axis_at), (shards_of,), jnp.float32, least / len(pieces), high / len(pieces))
        return jnp.repeat(jnp.exp(heights), extent[axis_at] // shards_of).reshape((-1,) + (1,) * (len(extent) - axis_at - 1))

    factor_of = one(*pieces[0])
    for cut in pieces[1:]:
        factor_of = factor_of * one(*cut)
    return factor_of


def deal_out(key, own, number, rows, amount, top, limit, skew):
    order = jax.random.permutation(key, amount)
    heavy_load, common = load_shares(amount, rows * top, limit, skew, True), load_shares(amount, rows * top, limit, skew, False)
    places = jnp.arange(amount)

    def named(sizes, offset_by):
        used = int((sizes > 0).sum())
        fixed = max(1, used // 4)
        shifted = fixed + (places - fixed + offset_by * (used - fixed)) % max(1, amount - fixed)
        return jnp.zeros((amount,), jnp.int32).at[order[jnp.where(places < fixed, places, shifted)]].set(jnp.asarray(sizes, jnp.int32))

    sizes = jnp.where(number % 4 == 0, named(heavy_load, number // 4), named(common, number - number // 4 - 1))
    mixed = jax.random.permutation(jax.random.fold_in(own, 3), amount)
    donor, taker = mixed[0:amount // 2 * 2:2], mixed[1:amount // 2 * 2:2]
    margin = jnp.minimum(sizes[donor] - 1, limit - sizes[taker]) // 2
    margin = jnp.where((donor == order[0]) | (taker == order[0]) | (sizes[taker] == 0), 0, jnp.maximum(margin, 0))
    shifted = jax.random.randint(jax.random.fold_in(own, 4), (amount // 2,), 0, 1 << 20) % (margin + 1)
    sizes = sizes.at[donor].add(-shifted).at[taker].add(shifted)
    members = jnp.searchsorted(jnp.cumsum(sizes), jnp.arange(rows * top), side="right").astype(jnp.int32)
    grid = members.reshape(top, rows).T
    grid = grid[jax.random.permutation(jax.random.fold_in(own, 1), rows)]
    offset_by = jax.random.randint(jax.random.fold_in(own, 2), (rows, 1), 0, top)
    return jnp.take_along_axis(grid, (jnp.arange(top)[None, :] + offset_by) % top, axis=1)


def load_shares(number_of, total, most, lean, full):
    portions = [(1 << 20) // math.isqrt(standing ** lean) + 1 for standing in range(1, number_of + 1)]
    largest = most if full else min(most, max(-(-total // number_of), total * portions[0] // sum(portions)))
    least = 1 if total - largest >= number_of - 1 else 0
    counts, surplus = [largest] + [least] * (number_of - 1), total - largest - least * (number_of - 1)
    while surplus > 0:
        candidates = [i for i in range(1, number_of) if counts[i] < largest] or [i for i in range(1, number_of) if counts[i] < most]
        pool, budget = sum([portions[i] for i in candidates]), surplus
        for i in candidates:
            extra = min(most - counts[i], max(1, budget * portions[i] // pool), surplus)
            counts[i] = counts[i] + extra
            surplus = surplus - extra
    return np.array(counts)


def bell_draw(rng, shape, scale, reach, pieces=(), held_as=jnp.bfloat16):
    array = scale * jax.random.normal(rng, shape, jnp.float32)
    if pieces:
        array = array * levels(rng, shape, pieces, -0.22, 0.18)
    return jnp.clip(array, -reach, reach).astype(held_as)


def setup_inputs(seed: int = 0) -> dict:
    keys = jax.random.split(jax.random.key(seed), 6)
    filterbank = bell_draw(keys[0], (NCH, NT), 1.0, 6.0, ((0, 256),))
    channel_mask = set_ends((jax.random.randint(keys[1], (NCH,), 0, 8) < 7).astype(jnp.int32), jax.random.fold_in(keys[1], 1), 0, 1)
    delays = set_ends(jax.random.randint(keys[2], (NDM, NSUB), 0, BLK), jax.random.fold_in(keys[2], 1), 0, BLK - 1).astype(jnp.int32)
    readers_keys = jax.random.split(jax.random.fold_in(keys[3], 1), NB * NACC // (NBD * NACC))
    readers_turns = jax.random.permutation(jax.random.fold_in(keys[3], 3), NB * NACC // (NBD * NACC))
    readers = jax.vmap(lambda own, number: deal_out(jax.random.fold_in(keys[3], 2), own, number, NBD * NACC, READERS, 1, CAP, 2))(readers_keys, readers_turns).reshape((NB, NACC, 1))
    stretch = jnp.clip(jnp.exp(jax.random.uniform(keys[4], (NACC,), jnp.float32, math.log(0.5), math.log(1.8))), 0.5, 1.8)
    return dict(filterbank=filterbank, channel_mask=channel_mask, delays=delays, readers=readers, stretch=stretch)


start_offset = 4.0
taper_half = 8.0


def sinc_table(stretch, width):
    row_pos = jnp.arange(2 * width, dtype=jnp.float32)[None, :, None]
    col_pos = jnp.arange(width, dtype=jnp.float32)[None, None, :]
    spread = row_pos - (start_offset + col_pos * stretch[:, None, None])
    taper = jnp.where(jnp.abs(spread) < taper_half, 0.5 + 0.5 * jnp.cos(math.pi * spread / taper_half), 0.0)
    return (jnp.sinc(spread) * taper).astype(jnp.bfloat16)


def reference(filterbank, channel_mask, delays, readers, stretch):
    channel_count, time_count = filterbank.shape
    masked = filterbank * channel_mask.astype(jnp.bfloat16)[:, None]
    band_count = channel_count // SUBCH
    selector = (jnp.arange(band_count)[:, None] == (jnp.arange(channel_count) // SUBCH)[None, :]).astype(jnp.bfloat16)
    sub = jnp.dot(selector, masked, preferred_element_type=jnp.float32).astype(jnp.bfloat16)
    sub_wide = lax.optimization_barrier(sub).astype(jnp.float32)
    sub_padded = jnp.concatenate([sub_wide, jnp.zeros((band_count, BLK), jnp.float32)], axis=1)

    def one_trial(delay_row):
        def one_band(band_row, delay_value):
            return lax.dynamic_slice_in_dim(band_row, delay_value.astype(jnp.int32), time_count)
        return jnp.sum(jax.vmap(one_band)(sub_padded, delay_row), axis=0)

    series = lax.map(one_trial, delays).astype(jnp.bfloat16)
    series_wide = lax.optimization_barrier(series).astype(jnp.float32)
    trial_count = series.shape[0]
    block_count = time_count // BLK
    padded = jnp.concatenate([series_wide, jnp.zeros((trial_count, BLK), jnp.float32)], axis=1)
    blocks = padded.reshape(trial_count, block_count + 1, BLK)
    window_slices = jnp.concatenate([blocks[:, :-1], blocks[:, 1:]], axis=2)
    resample_kernel = lax.optimization_barrier(sinc_table(stretch, BLK)).astype(jnp.float32)
    reader_ids = jnp.arange(N_TM, dtype=jnp.int32)

    def one_accel(acceleration_position):
        stretched_series = jnp.einsum("kqx,xr->qkr", window_slices, resample_kernel[acceleration_position], precision=lax.Precision.HIGHEST)
        nearest_sample = lax.optimization_barrier(stretched_series.astype(jnp.bfloat16)).astype(jnp.float32)
        match_tally = (readers[:, acceleration_position, 0][:, None] == reader_ids[None, :]).astype(jnp.float32)
        subband_totals = jnp.einsum("ye,yon->oen", match_tally, nearest_sample, precision=lax.Precision.HIGHEST)
        return subband_totals.reshape(trial_count, N_TM * BLK)

    stacked = lax.map(one_accel, jnp.arange(stretch.shape[0], dtype=jnp.int32))
    return series, stacked.astype(jnp.bfloat16)
```

```python
import functools
import math

import jax
import jax.numpy as jnp
from jax import lax
from jax.experimental import pallas as pl
from jax.experimental.pallas import tpu as pltpu
from jax.sharding import PartitionSpec as P

MESH = pl.DeviceIdType.MESH
BF, F32 = jnp.bfloat16, jnp.float32

BLK = 128
N_TM = 64
N_CHAN = 4
SHARD = 4096
ROWS = SHARD // BLK
PAIRS = N_TM // 2
OWN = 16
TRIALS = 8
NSUB = 64
NX = 4
NQ = 16
NACC = 8
SENT = TRIALS * ROWS + 16
CHUNK = 4
START_OFFSET = 4.0
TAPER_HALF = 8.0


def remote(src, dst, send_sem, recv_sem, tm, chan):
    return pltpu.make_async_remote_copy(
        src_ref=src,
        dst_ref=dst,
        send_sem=send_sem,
        recv_sem=recv_sem,
        device_id=(tm, chan),
        device_id_type=MESH,
    )


def subband_kernel(
    fb, mask, delays,
    sub_all, halo_all, delays_all,
    fb_v, lhs_v, for_core, from_core, staged, parts, halo_f, halo_v,
    load_sem, core_send, core_recv, part_send, part_recv,
    sub_send, sub_recv, halo_send, halo_recv, delay_send, delay_recv,
):
    t, c = lax.axis_index("tm"), lax.axis_index("chan")
    core, me = t % 2, t // 2
    other = t + 1 - 2 * core

    def shard_at(n, parity):
        return 2 * ((me + 1 + n) % PAIRS) + parity

    def load(n, parity, slot):
        at = pl.ds(pl.multiple_of(shard_at(n, parity) * SHARD, SHARD), SHARD)
        return pltpu.make_async_copy(fb.at[:, at], fb_v.at[:, at], load_sem.at[slot])

    def start_other(n, carry):
        load(n, 1 - core, n).start()
        return carry

    def start_own(n, carry):
        load(n, core, PAIRS + n).start()
        return carry

    lax.fori_loop(0, PAIRS, start_other, 0)
    lax.fori_loop(0, PAIRS, start_own, 0)

    barrier = pltpu.get_barrier_semaphore()

    def greet(tm, chan):
        pl.semaphore_signal(barrier, inc=1, device_id=(tm, chan), device_id_type=MESH)

    def greet_plane(n, carry):
        greet(2 * ((me + 1 + n) % PAIRS) + core, c)
        return carry

    lax.fori_loop(0, PAIRS - 1, greet_plane, 0)
    for step in range(1, N_CHAN):
        greet(t, (c + step) % N_CHAN)

    @pl.when(t > 0)
    def _():
        for chan in range(N_CHAN):
            greet(t - 1, chan)

    @pl.when(t < N_TM - 1)
    def _():
        for chan in range(N_CHAN):
            greet(t + 1, chan)

    lane = lax.broadcasted_iota(jnp.int32, (16, 16 * OWN), 1)
    row = lax.broadcasted_iota(jnp.int32, (16, 16 * OWN), 0)
    weights = jnp.zeros((16, 16 * OWN), F32)
    for channel in range(OWN):
        value = mask[channel].astype(F32)
        weights = jnp.where((lane // OWN == row) & (lane % OWN == channel), value, weights)
    lhs_v[...] = weights.astype(BF)

    def shard_sum(shard):
        halves = []
        for half in range(2):
            at = pl.multiple_of(shard * SHARD + half * (SHARD // 2), SHARD // 2)
            block = fb_v[:, pl.ds(at, SHARD // 2)]
            halves.append(
                jnp.concatenate([block[:, i * BLK:(i + 1) * BLK] for i in range(16)], axis=0)
            )
        total = jnp.dot(
            lhs_v[...], jnp.concatenate(halves, axis=1), preferred_element_type=F32
        )
        return jnp.concatenate([total[:, :BLK], total[:, BLK:]], axis=0)

    def to_core(chunk):
        rows = pl.ds(chunk * CHUNK, CHUNK)
        return remote(
            for_core.at[rows], from_core.at[rows],
            core_send.at[chunk], core_recv.at[chunk], other, c,
        )

    pl.semaphore_wait(
        barrier,
        PAIRS - 1 + N_CHAN - 1
        + N_CHAN * (t > 0).astype(jnp.int32)
        + N_CHAN * (t < N_TM - 1).astype(jnp.int32),
    )

    def delay_copy(step):
        return remote(
            delays, delays_all.at[c], delay_send.at[step - 1], delay_recv.at[c],
            t, (c + step) % N_CHAN,
        )

    for step in range(1, N_CHAN):
        delay_copy(step).start()
    delays_all[c] = delays[...]

    def sum_other(chunk, carry):
        for i in range(CHUNK):
            n = chunk * CHUNK + i
            load(n, 1 - core, n).wait()
            for_core[n] = shard_sum(shard_at(n, 1 - core)).astype(BF)
        to_core(chunk).start()
        return carry

    lax.fori_loop(0, PAIRS // CHUNK, sum_other, 0)

    def send_part(n):
        return remote(
            staged.at[n], parts.at[me], part_send.at[n], part_recv.at[me],
            shard_at(n, core), c,
        )

    def sum_own(chunk, carry):
        to_core(chunk).wait_recv()
        for i in range(CHUNK):
            n = chunk * CHUNK + i
            load(n, core, PAIRS + n).wait()
            total = shard_sum(shard_at(n, core)) + from_core[n].astype(F32)
            staged[n] = total.astype(BF)

            @pl.when(n < PAIRS - 1)
            def _():
                send_part(n).start()

        return carry

    lax.fori_loop(0, PAIRS // CHUNK, sum_own, 0)
    parts[me] = staged[PAIRS - 1]

    def part_arrival(j):
        return remote(parts.at[j], parts.at[j], part_send.at[0], part_recv.at[j], other, c)

    for k in range(OWN):
        for j in (2 * k, 2 * k + 1):
            @pl.when(j != me)
            def _():
                part_arrival(j).wait_recv()
        total = parts[2 * k].astype(F32) + parts[2 * k + 1].astype(F32)
        sub_all[c, k * ROWS:(k + 1) * ROWS] = total.astype(BF)
        halo_f[2 * k:2 * k + 2] = total[:2]
    halo_v[...] = halo_f[...].astype(BF)

    def sub_copy(step):
        return remote(
            sub_all.at[c], sub_all.at[c], sub_send.at[step - 1], sub_recv.at[c],
            t, (c + step) % N_CHAN,
        )

    def halo_copy(chan):
        return remote(
            halo_v, halo_all.at[c], halo_send.at[chan], halo_recv.at[c], t - 1, chan
        )

    for step in (2, 1, 3):
        sub_copy(step).start()

    @pl.when(t > 0)
    def _():
        for chan in range(N_CHAN):
            halo_copy(chan).start()

    @pl.when(t == N_TM - 1)
    def _():
        halo_all[...] = jnp.zeros_like(halo_all)

    def sent_core(chunk, carry):
        to_core(chunk).wait_send()
        return carry

    def sent_part(n, carry):
        send_part(n).wait_send()
        return carry

    lax.fori_loop(0, PAIRS // CHUNK, sent_core, 0)
    lax.fori_loop(0, PAIRS - 1, sent_part, 0)
    for step in range(1, N_CHAN):
        delay_copy(step).wait_send()
        source = (c + step) % N_CHAN
        remote(
            delays, delays_all.at[source], delay_send.at[0], delay_recv.at[source], t, source
        ).wait_recv()

    @pl.when(t < N_TM - 1)
    def _():
        for chan in range(N_CHAN):
            remote(
                halo_v, halo_all.at[chan], halo_send.at[0], halo_recv.at[chan], t + 1, chan
            ).wait_recv()

    @pl.when(t > 0)
    def _():
        for chan in range(N_CHAN):
            halo_copy(chan).wait_send()

    for step in range(1, N_CHAN):
        source = (c + step) % N_CHAN
        remote(
            sub_all.at[source], sub_all.at[source], sub_send.at[0], sub_recv.at[source],
            t, source,
        ).wait_recv()
        sub_copy(step).wait_send()


def subbands(filterbank, channel_mask, delays):
    vmem = pl.BlockSpec(memory_space=pltpu.VMEM)
    dma = pltpu.SemaphoreType.DMA
    return pl.pallas_call(
        subband_kernel,
        out_shape=(
            jax.ShapeDtypeStruct((N_CHAN, OWN * ROWS, BLK), BF),
            jax.ShapeDtypeStruct((N_CHAN, 2 * OWN, BLK), BF),
            jax.ShapeDtypeStruct((N_CHAN,) + delays.shape, jnp.int32),
        ),
        in_specs=[
            pl.BlockSpec(memory_space=pl.ANY),
            pl.BlockSpec(memory_space=pltpu.SMEM),
            vmem,
        ],
        out_specs=(vmem, vmem, vmem),
        scratch_shapes=[
            pltpu.VMEM(filterbank.shape, BF),
            pltpu.VMEM((16, 16 * OWN), BF),
            pltpu.VMEM((PAIRS, ROWS, BLK), BF),
            pltpu.VMEM((PAIRS, ROWS, BLK), BF),
            pltpu.VMEM((PAIRS, ROWS, BLK), BF),
            pltpu.VMEM((PAIRS, ROWS, BLK), BF),
            pltpu.VMEM((2 * OWN, BLK), F32),
            pltpu.VMEM((2 * OWN, BLK), BF),
            dma((N_TM,)),
            dma((PAIRS // CHUNK,)),
            dma((PAIRS // CHUNK,)),
            dma((PAIRS,)),
            dma((PAIRS,)),
            dma((N_CHAN,)),
            dma((N_CHAN,)),
            dma((N_CHAN,)),
            dma((N_CHAN,)),
            dma((N_CHAN,)),
            dma((N_CHAN,)),
        ],
        compiler_params=pltpu.CompilerParams(
            collective_id=0, has_side_effects=True, vmem_limit_bytes=24 * 2**20
        ),
        name="subbands",
    )(filterbank, channel_mask, delays)


def dedisperse_kernel(sub_all, halo_all, delays_all, series, rows, wide, halo_f, turned, halo_rows):
    c = lax.axis_index("chan")
    for chan in range(N_CHAN):
        halo_f[chan] = halo_all[chan].astype(F32)
    for k in range(NSUB):
        chan, own = k // OWN, k % OWN
        wide[k, :ROWS] = sub_all[chan, own * ROWS:(own + 1) * ROWS].astype(F32)
        wide[k, ROWS:ROWS + 2] = halo_f[chan, 2 * own:2 * own + 2]
    lane = lax.broadcasted_iota(jnp.int32, (1, BLK), 1)
    tall = ROWS + 8

    def one_band(k, totals):
        lower = wide[k, 0:tall]
        upper = wide[k, 1:tall + 1]
        out = []
        for m in range(TRIALS):
            delay = delays_all[k // OWN, c * TRIALS + m, k % OWN]
            joined = jnp.where(lane >= delay, lower, upper)
            out.append(totals[m] + pltpu.roll(joined, (BLK - delay) % BLK, 1))
        return tuple(out)

    totals = lax.fori_loop(
        0, NSUB, one_band, tuple(jnp.zeros((tall, BLK), F32) for _ in range(TRIALS))
    )
    halo_rows[...] = jnp.zeros_like(halo_rows)
    for m in range(TRIALS):
        rows[m * ROWS:(m + 1) * ROWS] = totals[m][:ROWS].astype(BF)
        halo_rows[m:m + 1] = totals[m][ROWS:ROWS + 1]
        turned[pl.ds(m, ROWS, stride=TRIALS)] = totals[m][:ROWS]
    rows[TRIALS * ROWS:] = halo_rows[...].astype(BF)
    for b in range(ROWS):
        series[:, b * BLK:(b + 1) * BLK] = turned[b * TRIALS:(b + 1) * TRIALS].astype(BF)


def dedisperse(sub_all, halo_all, delays_all):
    vmem = pl.BlockSpec(memory_space=pltpu.VMEM)
    return pl.pallas_call(
        dedisperse_kernel,
        out_shape=(
            jax.ShapeDtypeStruct((TRIALS, SHARD), BF),
            jax.ShapeDtypeStruct((SENT, BLK), BF),
        ),
        in_specs=[vmem, vmem, pl.BlockSpec(memory_space=pltpu.SMEM)],
        out_specs=(vmem, vmem),
        scratch_shapes=[
            pltpu.VMEM((NSUB, ROWS + 16, BLK), F32),
            pltpu.VMEM((N_CHAN, 2 * OWN, BLK), F32),
            pltpu.VMEM((TRIALS * ROWS, BLK), F32),
            pltpu.VMEM((16, BLK), F32),
        ],
        compiler_params=pltpu.CompilerParams(vmem_limit_bytes=16 * 2**20),
        name="dedisperse",
    )(sub_all, halo_all, delays_all)


def sinc_table(stretch_value):
    col = lax.broadcasted_iota(jnp.int32, (8, BLK), 1).astype(F32)
    centre = START_OFFSET + col * stretch_value
    whole = jnp.round(centre)
    odd = whole - 2.0 * jnp.floor(whole * 0.5)
    wave = (2.0 * odd - 1.0) * jnp.sin(math.pi * (centre - whole)) / math.pi
    angle = (math.pi / TAPER_HALF) * (centre - 16.0 * jnp.floor(centre / 16.0))
    cos_p, sin_p = 0.5 * jnp.cos(angle), 0.5 * jnp.sin(angle)
    pieces = []
    row = lax.broadcasted_iota(jnp.int32, (8, BLK), 0)
    sign = (1 - 2 * (row % 2)).astype(F32)
    signed_wave = sign * wave
    tapers = []
    for half in range(2):
        turn = (math.pi / TAPER_HALF) * (row + 8 * half).astype(F32)
        tapers.append(0.5 + jnp.cos(turn) * cos_p + jnp.sin(turn) * sin_p)
    for group in range(2 * BLK // 8):
        x = (row + 8 * group).astype(F32) - centre
        sinc = jnp.where(x == 0.0, 1.0, signed_wave / jnp.where(x == 0.0, 1.0, x))
        pieces.append(jnp.where(jnp.abs(x) < TAPER_HALF, sinc * tapers[group % 2], 0.0))
    return jnp.concatenate(pieces, axis=0).astype(BF)


def stack_kernel(
    rows, readers, stretch,
    stacked,
    gathered, readers_all, table, tall, grouped, outgoing, arrived,
    row_send, row_recv, reader_send, reader_recv, out_send, out_recv,
):
    t, c = lax.axis_index("tm"), lax.axis_index("chan")
    x, q = t // NQ, t % NQ
    barrier = pltpu.get_barrier_semaphore()

    def greet(tm):
        pl.semaphore_signal(barrier, inc=1, device_id=(tm, c), device_id_type=MESH)

    for step in range(1, NX):
        greet(((x + step) % NX) * NQ + q)
    for step in range(1, NQ):
        greet(x * NQ + (q + step) % NQ)
    pl.semaphore_wait(barrier, NX - 1 + NQ - 1)

    def row_copy(step):
        return remote(
            rows, gathered.at[x], row_send.at[step - 1], row_recv.at[x],
            ((x + step) % NX) * NQ + q, c,
        )

    def reader_copy(step):
        return remote(
            readers, readers_all.at[x], reader_send.at[step - 1], reader_recv.at[x],
            ((x + step) % NX) * NQ + q, c,
        )

    for step in (2, 1, 3):
        row_copy(step).start()
    for step in (2, 1, 3):
        reader_copy(step).start()
    gathered[x] = rows[...]
    readers_all[x] = readers[...]

    def one_table(a, carry):
        table[a] = sinc_table(stretch[a])
        return carry

    lax.fori_loop(0, NACC, one_table, 0)

    for step in range(1, NX):
        source = (x + step) % NX
        remote(
            readers, readers_all.at[source], reader_send.at[0], reader_recv.at[source],
            source * NQ + q, c,
        ).wait_recv()
    lane = lax.broadcasted_iota(jnp.int32, (ROWS, BLK), 1)
    chosen = []
    for source in range(NX):
        names = readers_all[source]
        wanted = jnp.zeros((ROWS, BLK), jnp.int32)
        for a in range(NACC):
            wanted = jnp.where(lane // NQ == a, names[:, a:a + 1], wanted)
        chosen.append((wanted == x * NQ + lane % NQ).astype(F32))
    pick = jnp.concatenate(chosen, axis=0).T.astype(BF)

    for step in range(1, NX):
        source = (x + step) % NX
        remote(
            rows, gathered.at[source], row_send.at[0], row_recv.at[source],
            source * NQ + q, c,
        ).wait_recv()
    for source in range(NX):
        last = gathered[source, TRIALS * ROWS:].astype(F32)
        for m in range(TRIALS):
            tall[m, source, :ROWS] = gathered[source, m * ROWS:(m + 1) * ROWS].astype(F32)
            tall[m, source, ROWS:ROWS + 1] = last[m:m + 1]
    for m in range(TRIALS):
        for half in range(2):
            block = jnp.concatenate(
                [tall[m, source, half:half + ROWS] for source in range(NX)], axis=0
            ).astype(BF)
            sums = jnp.dot(pick, block, preferred_element_type=F32)
            for a in range(NACC):
                grouped[a, half, pl.ds(m, NQ, stride=TRIALS)] = sums[a * NQ:(a + 1) * NQ]

    def two_accelerations(pair, carry):
        results = []
        for i in range(2):
            a = 2 * pair + i
            block = jnp.concatenate([grouped[a, 0], grouped[a, 1]], axis=1).astype(BF)
            results.append(jnp.dot(block, table[a], preferred_element_type=F32))
        for reader in range(NQ):
            at = slice(reader * TRIALS, (reader + 1) * TRIALS)
            outgoing[reader, pl.ds(pl.multiple_of(pair * 16, 16), 16)] = jnp.concatenate(
                [results[0][at], results[1][at]], axis=0
            ).astype(BF)
        return carry

    lax.fori_loop(0, NACC // 2, two_accelerations, 0)

    def out_copy(step):
        target = (q + step) % NQ
        return remote(
            outgoing.at[target], arrived.at[q], out_send.at[step - 1], out_recv.at[q],
            x * NQ + target, c,
        )

    for step in range(1, NQ):
        out_copy(step).start()
    total = outgoing[q].astype(F32)
    for step in range(1, NQ):
        source = (q + step) % NQ
        remote(
            outgoing.at[0], arrived.at[source], out_send.at[0], out_recv.at[source],
            x * NQ + source, c,
        ).wait_recv()
        total = total + arrived[source].astype(F32)
    for a in range(NACC):
        stacked[a] = total[a * TRIALS:(a + 1) * TRIALS].astype(BF)
    for step in range(1, NQ):
        out_copy(step).wait_send()
    for step in range(1, NX):
        row_copy(step).wait_send()
        reader_copy(step).wait_send()


def stack(rows, readers, stretch):
    vmem = pl.BlockSpec(memory_space=pltpu.VMEM)
    dma = pltpu.SemaphoreType.DMA
    return pl.pallas_call(
        stack_kernel,
        out_shape=jax.ShapeDtypeStruct((NACC, TRIALS, BLK), BF),
        in_specs=[vmem, vmem, pl.BlockSpec(memory_space=pltpu.SMEM)],
        out_specs=vmem,
        scratch_shapes=[
            pltpu.VMEM((NX, SENT, BLK), BF),
            pltpu.VMEM((NX, ROWS, NACC), jnp.int32),
            pltpu.VMEM((NACC, 2 * BLK, BLK), BF),
            pltpu.VMEM((TRIALS, NX, ROWS + 8, BLK), F32),
            pltpu.VMEM((NACC, 2, TRIALS * NQ, BLK), F32),
            pltpu.VMEM((NQ, NACC * TRIALS, BLK), BF),
            pltpu.VMEM((NQ, NACC * TRIALS, BLK), BF),
            dma((NX,)),
            dma((NX,)),
            dma((NX,)),
            dma((NX,)),
            dma((NQ,)),
            dma((NQ,)),
        ],
        compiler_params=pltpu.CompilerParams(
            collective_id=1, has_side_effects=True, vmem_limit_bytes=16 * 2**20
        ),
        name="stack",
    )(rows, readers, stretch)


def on_device(filterbank, channel_mask, delays, readers, stretch):
    sub_all, halo_all, delays_all = subbands(filterbank, channel_mask, delays)
    series, rows = dedisperse(sub_all, halo_all, delays_all)
    stacked = stack(rows, readers.reshape(ROWS, NACC), stretch)
    return series, stacked


def solution(mesh):
    return jax.shard_map(
        on_device,
        mesh=mesh,
        in_specs=(
            P(("chan", "tm"), None),
            P(("chan", "tm")),
            P(None, "chan"),
            P("tm", None, None),
            P(),
        ),
        out_specs=(P("chan", "tm"), P(None, "chan", "tm")),
        check_vma=False,
    )
```

```python
import math

import jax
import jax.numpy as jnp
from jax import lax
from jax.experimental import pallas as pl
from jax.experimental.pallas import tpu as pltpu
from jax.sharding import PartitionSpec as P

MESH = pl.DeviceIdType.MESH
BF, F32 = jnp.bfloat16, jnp.float32

BLK = 128
N_TM = 64
N_CHAN = 4
SHARD = 4096
ROWS = SHARD // BLK
PAIRS = N_TM // 2
OWN = 16
TRIALS = 8
NX = 4
NQ = 16
NACC = 8
GROUP = 32
LANE_GROUPS = BLK // GROUP
STEPS = 4
REACH = GROUP * (STEPS + 1)
CHUNK = 4
START_OFFSET = 4.0
TAPER_HALF = 8.0


def remote(src, dst, send_sem, recv_sem, tm, chan):
    return pltpu.make_async_remote_copy(
        src_ref=src,
        dst_ref=dst,
        send_sem=send_sem,
        recv_sem=recv_sem,
        device_id=(tm, chan),
        device_id_type=MESH,
    )


def sinc_table(stretch_value):
    col = lax.broadcasted_iota(jnp.int32, (8, BLK), 1).astype(F32)
    centre = START_OFFSET + col * stretch_value
    whole = jnp.round(centre)
    odd = whole - 2.0 * jnp.floor(whole * 0.5)
    wave = (2.0 * odd - 1.0) * jnp.sin(math.pi * (centre - whole)) / math.pi
    angle = (math.pi / TAPER_HALF) * (centre - 16.0 * jnp.floor(centre / 16.0))
    cos_p, sin_p = 0.5 * jnp.cos(angle), 0.5 * jnp.sin(angle)
    pieces = []
    row = lax.broadcasted_iota(jnp.int32, (8, BLK), 0)
    sign = (1 - 2 * (row % 2)).astype(F32)
    signed_wave = sign * wave
    tapers = []
    for half in range(2):
        turn = (math.pi / TAPER_HALF) * (row + 8 * half).astype(F32)
        tapers.append(0.5 + jnp.cos(turn) * cos_p + jnp.sin(turn) * sin_p)
    for group in range(2 * BLK // 8):
        x = (row + 8 * group).astype(F32) - centre
        sinc = jnp.where(x == 0.0, 1.0, signed_wave / jnp.where(x == 0.0, 1.0, x))
        pieces.append(jnp.where(jnp.abs(x) < TAPER_HALF, sinc * tapers[group % 2], 0.0))
    return jnp.concatenate(pieces, axis=0).astype(BF)


def turn(blocks):
    lane_group = lax.broadcasted_iota(jnp.int32, (ROWS, BLK), 1) // GROUP
    stacked = []
    for g in range(LANE_GROUPS):
        merged = blocks[0]
        for i in range(LANE_GROUPS):
            shift = (i - g) * GROUP % BLK
            moved = pltpu.roll(blocks[i], shift, 1) if shift else blocks[i]
            merged = moved if i == 0 else jnp.where(lane_group == i, moved, merged)
        stacked.append(merged)
    return jnp.concatenate(stacked, axis=0).T


def turn_back(rows):
    lane_group = lax.broadcasted_iota(jnp.int32, (ROWS, BLK), 1) // GROUP
    flipped = rows.T
    out = []
    for i in range(LANE_GROUPS):
        merged = None
        for g in range(LANE_GROUPS):
            piece = flipped[g * ROWS:(g + 1) * ROWS]
            shift = (g - i) * GROUP % BLK
            moved = pltpu.roll(piece, shift, 1) if shift else piece
            merged = moved if g == 0 else jnp.where(lane_group == g, moved, merged)
        out.append(merged)
    return out


def lane_steps():
    shape = (2 * BLK, STEPS * BLK)
    row = lax.broadcasted_iota(jnp.int32, shape, 0)
    col = lax.broadcasted_iota(jnp.int32, shape, 1)
    group = (col % BLK) // GROUP + col // BLK + 1
    block = col % GROUP + group // LANE_GROUPS
    group = group % LANE_GROUPS
    inside = (row == group * GROUP + block) & (block < ROWS)
    beyond = (row // GROUP == LANE_GROUPS + group) & (block == ROWS)
    return jnp.where(inside | beyond, 1.0, 0.0).astype(BF)


def kernel(
    fb, mask_in, delays_in, readers_in, stretch_in,
    series, stacked,
    fb_v, mask, stretch, delays_v, readers_v, delays_all, delays_s, readers_all,
    for_core, from_core, staged, parts, halo_f, halo_v, halo_all, sub_all, steps, reach,
    table, turned, rows, first, gathered, first_all, tall, grouped, outgoing, arrived,
    small_sem, load_sem, core_send, core_recv, part_send, part_recv,
    sub_send, sub_recv, halo_send, halo_recv, delay_send, delay_recv, delay_in,
    reader_send, reader_recv, row_send, row_recv, first_send, first_recv, out_send, out_recv,
):
    t, c = lax.axis_index("tm"), lax.axis_index("chan")
    core, me = t % 2, t // 2
    other = t + 1 - 2 * core
    x, q = t // NQ, t % NQ

    small = [
        pltpu.make_async_copy(source, target, small_sem.at[i])
        for i, (source, target) in enumerate(
            ((mask_in, mask), (delays_in, delays_v), (readers_in, readers_v), (stretch_in, stretch))
        )
    ]
    for copy in small:
        copy.start()

    def shard_at(n, parity):
        return 2 * ((me + 1 + n) % PAIRS) + parity

    def load(n, parity, slot):
        at = pl.ds(pl.multiple_of(shard_at(n, parity) * SHARD, SHARD), SHARD)
        return pltpu.make_async_copy(fb.at[:, at], fb_v.at[:, at], load_sem.at[slot])

    def start_other(n, carry):
        load(n, 1 - core, n).start()
        return carry

    def start_own(n, carry):
        load(n, core, PAIRS + n).start()
        return carry

    lax.fori_loop(0, PAIRS, start_other, 0)
    lax.fori_loop(0, PAIRS, start_own, 0)

    barrier = pltpu.get_barrier_semaphore()

    def greet(tm, chan):
        pl.semaphore_signal(barrier, inc=1, device_id=(tm, chan), device_id_type=MESH)

    def greet_plane(n, carry):
        greet((t + 1 + n) % N_TM, c)
        return carry

    lax.fori_loop(0, N_TM - 1, greet_plane, 0)
    for step in range(1, N_CHAN):
        greet(t, (c + step) % N_CHAN)

    @pl.when(t > 0)
    def _():
        for step in range(1, N_CHAN):
            greet(t - 1, (c + step) % N_CHAN)

    @pl.when(t < N_TM - 1)
    def _():
        for step in range(1, N_CHAN):
            greet(t + 1, (c + step) % N_CHAN)

    for copy in small:
        copy.wait()
    sublane = lax.broadcasted_iota(jnp.int32, (8, BLK), 0)
    weights = []
    for half in range(2):
        value = jnp.zeros((8, BLK), F32)
        for i in range(8):
            value = jnp.where(sublane == i, mask[8 * half + i].astype(F32), value)
        weights.append(value)

    def block_sum(at):
        block = fb_v[:, pl.ds(at, BLK)].astype(F32)
        return block[:8] * weights[0] + block[8:] * weights[1]

    def merge(blocks):
        step = 1
        while len(blocks) > 1:
            even = (sublane // step) % 2 == 0
            blocks = [
                jnp.where(even, a, b) + pltpu.roll(jnp.where(even, b, a), 8 - step, 0)
                for a, b in zip(blocks[0::2], blocks[1::2])
            ]
            step *= 2
        return blocks[0]

    def shard_sum(shard):
        base = pl.multiple_of(shard * SHARD, SHARD)
        return jnp.concatenate(
            [
                merge([block_sum(base + (8 * group + i) * BLK) for i in range(8)])
                for group in range(ROWS // 8)
            ],
            axis=0,
        )

    def to_core(chunk):
        at = pl.ds(chunk * CHUNK, CHUNK)
        return remote(
            for_core.at[at], from_core.at[at],
            core_send.at[chunk], core_recv.at[chunk], other, c,
        )

    pl.semaphore_wait(
        barrier,
        N_TM - 1 + N_CHAN - 1
        + (N_CHAN - 1) * ((t > 0).astype(jnp.int32) + (t < N_TM - 1).astype(jnp.int32)),
    )

    def delay_copy(step):
        return remote(
            delays_v, delays_all.at[c], delay_send.at[step - 1], delay_recv.at[c],
            t, (c + step) % N_CHAN,
        )

    def reader_copy(step):
        return remote(
            readers_v, readers_all.at[x], reader_send.at[step - 1], reader_recv.at[x],
            ((x + step) % NX) * NQ + q, c,
        )

    for step in range(1, N_CHAN):
        delay_copy(step).start()
    for step in range(1, NX):
        reader_copy(step).start()
    delays_all[c] = delays_v[...]
    readers_all[x] = readers_v[...]

    def sum_other(chunk, carry):
        for i in range(CHUNK):
            n = chunk * CHUNK + i
            load(n, 1 - core, n).wait()
            for_core[n] = shard_sum(shard_at(n, 1 - core))
        to_core(chunk).start()
        return carry

    lax.fori_loop(0, PAIRS // CHUNK, sum_other, 0)

    def send_part(n):
        return remote(
            staged.at[n], parts.at[me], part_send.at[n], part_recv.at[me],
            shard_at(n, core), c,
        )

    def sum_own(chunk, carry):
        to_core(chunk).wait_recv()
        for i in range(CHUNK):
            n = chunk * CHUNK + i
            load(n, core, PAIRS + n).wait()
            staged[n] = (shard_sum(shard_at(n, core)) + from_core[n]).astype(BF)

            @pl.when(n < PAIRS - 1)
            def _():
                send_part(n).start()

        return carry

    lax.fori_loop(0, PAIRS // CHUNK, sum_own, 0)
    parts[me] = staged[PAIRS - 1]

    def one_table(a, carry):
        table[a] = sinc_table(stretch[a])
        return carry

    lax.fori_loop(0, NACC, one_table, 0)
    steps[...] = lane_steps()
    halo_f[...] = jnp.zeros_like(halo_f)
    for step in range(1, N_CHAN):
        source = (c + step) % N_CHAN
        remote(
            delays_v, delays_all.at[source], delay_send.at[0], delay_recv.at[source], t, source
        ).wait_recv()
    delay_local = pltpu.make_async_copy(delays_all, delays_s, delay_in)
    delay_local.start()
    for step in range(1, NX):
        source = (x + step) % NX
        remote(
            readers_v, readers_all.at[source], reader_send.at[0], reader_recv.at[source],
            source * NQ + q, c,
        ).wait_recv()
    names = jnp.concatenate([readers_all[source][:, 0, :] for source in range(NX)], axis=1)
    reader_row = lax.broadcasted_iota(jnp.int32, (NQ, BLK), 0) + x * NQ
    pick = jnp.concatenate(
        [(names[a:a + 1] == reader_row).astype(F32) for a in range(NACC)], axis=0
    ).astype(BF)
    delay_local.wait()

    def part_arrival(j):
        return remote(parts.at[j], parts.at[j], part_send.at[0], part_recv.at[j], other, c)

    for stack in range(OWN // LANE_GROUPS):
        blocks = []
        for i in range(LANE_GROUPS):
            k = stack * LANE_GROUPS + i
            for j in (2 * k, 2 * k + 1):
                @pl.when(j != me)
                def _():
                    part_arrival(j).wait_recv()
            total = parts[2 * k].astype(F32) + parts[2 * k + 1].astype(F32)
            halo_f[k:k + 1] = total[:1]
            blocks.append(total)
        sub_all[c, stack * BLK:(stack + 1) * BLK] = turn(blocks).astype(BF)

    def sub_copy(step):
        return remote(
            sub_all.at[c], sub_all.at[c], sub_send.at[step - 1], sub_recv.at[c],
            t, (c + step) % N_CHAN,
        )

    def halo_copy(chan):
        return remote(
            halo_v, halo_all.at[c], halo_send.at[chan], halo_recv.at[c], t - 1, chan
        )

    for step in (2, 1, 3):
        sub_copy(step).start()
    first_blocks = halo_f[...]
    halo_v[...] = jnp.concatenate(
        [first_blocks] + [pltpu.roll(first_blocks, BLK - g * GROUP, 1) for g in range(1, LANE_GROUPS)],
        axis=0,
    ).T[:GROUP].astype(BF)

    @pl.when(t > 0)
    def _():
        for chan in range(N_CHAN):
            halo_copy(chan).start()

    @pl.when(t == N_TM - 1)
    def _():
        halo_all[...] = jnp.zeros_like(halo_all)

    @pl.when(t < N_TM - 1)
    def _():
        for chan in range(N_CHAN):
            remote(
                halo_v, halo_all.at[chan], halo_send.at[0], halo_recv.at[chan], t + 1, chan
            ).wait_recv()

    lane = lax.broadcasted_iota(jnp.int32, (GROUP, BLK), 1)
    totals = tuple(jnp.zeros((GROUP, BLK), F32) for _ in range(TRIALS))
    for step in (0, 1, 3, 2):
        source = (c + step) % N_CHAN
        if step:
            remote(
                sub_all.at[source], sub_all.at[source], sub_send.at[0], sub_recv.at[source],
                t, source,
            ).wait_recv()
        beyond = halo_all[source].astype(F32)

        def extend(k, carry):
            at = pl.ds(pl.multiple_of(k * GROUP, GROUP), GROUP)
            own = sub_all[source, at]
            next_blocks = jnp.where(lane % GROUP == k, beyond, 0.0).astype(BF)
            moved = jnp.dot(
                jnp.concatenate([own, next_blocks], axis=1), steps[...],
                preferred_element_type=F32,
            )
            reach[k, :GROUP] = own.astype(F32)
            for e in range(STEPS):
                reach[k, (e + 1) * GROUP:(e + 2) * GROUP] = moved[:, e * BLK:(e + 1) * BLK]
            return carry

        lax.fori_loop(0, OWN, extend, 0, unroll=4)

        def one_band(k, sums):
            return tuple(
                sums[m] + reach[k, pl.ds(delays_s[source, k, c * TRIALS + m], GROUP)]
                for m in range(TRIALS)
            )

        totals = lax.fori_loop(0, OWN, one_band, totals)

    for pair in range(TRIALS // LANE_GROUPS):
        back = turn_back(
            jnp.concatenate(totals[pair * LANE_GROUPS:(pair + 1) * LANE_GROUPS], axis=0)
        )
        for i in range(LANE_GROUPS):
            m = pair * LANE_GROUPS + i
            rows[m * ROWS:(m + 1) * ROWS] = back[i].astype(BF)
            turned[pl.ds(m, ROWS, stride=TRIALS)] = back[i]
    first[...] = jnp.concatenate([turned[:TRIALS], jnp.zeros((TRIALS, BLK), F32)], axis=0).astype(BF)

    def row_copy(step):
        return remote(
            rows, gathered.at[x], row_send.at[step - 1], row_recv.at[x],
            ((x + step) % NX) * NQ + q, c,
        )

    def first_copy(target):
        return remote(
            first, first_all.at[(t - 1) // NQ], first_send.at[target],
            first_recv.at[(t - 1) // NQ], target * NQ + (t - 1) % NQ, c,
        )

    for step in (2, 1, 3):
        row_copy(step).start()

    @pl.when(t > 0)
    def _():
        for target in range(NX):
            first_copy(target).start()

    gathered[x] = rows[...]
    for b in range(ROWS):
        series[:, b * BLK:(b + 1) * BLK] = turned[b * TRIALS:(b + 1) * TRIALS].astype(BF)

    def first_arrival(source):
        return remote(
            first, first_all.at[source], first_send.at[0], first_recv.at[source],
            source * NQ + q + 1, c,
        )

    for source in range(NX - 1):
        first_arrival(source).wait_recv()

    @pl.when(q < NQ - 1)
    def _():
        first_arrival(NX - 1).wait_recv()

    @pl.when(q == NQ - 1)
    def _():
        first_all[NX - 1] = jnp.zeros((16, BLK), BF)

    for step in range(1, NX):
        source = (x + step) % NX
        remote(
            rows, gathered.at[source], row_send.at[0], row_recv.at[source],
            source * NQ + q, c,
        ).wait_recv()

    for source in range(NX):
        last = first_all[source].astype(F32)
        for m in range(TRIALS):
            tall[m, source, :ROWS] = gathered[source, m * ROWS:(m + 1) * ROWS].astype(F32)
            tall[m, source, ROWS:ROWS + 1] = last[m:m + 1]
    for m in range(TRIALS):
        for half in range(2):
            block = jnp.concatenate(
                [tall[m, source, half:half + ROWS] for source in range(NX)], axis=0
            ).astype(BF)
            sums = jnp.dot(pick, block, preferred_element_type=F32)
            for a in range(NACC):
                grouped[a, half, pl.ds(m, NQ, stride=TRIALS)] = sums[a * NQ:(a + 1) * NQ]

    def two_accelerations(pair, carry):
        results = []
        for i in range(2):
            a = 2 * pair + i
            block = jnp.concatenate([grouped[a, 0], grouped[a, 1]], axis=1).astype(BF)
            results.append(jnp.dot(block, table[a], preferred_element_type=F32))
        for reader in range(NQ):
            at = slice(reader * TRIALS, (reader + 1) * TRIALS)
            outgoing[reader, pl.ds(pl.multiple_of(pair * 16, 16), 16)] = jnp.concatenate(
                [results[0][at], results[1][at]], axis=0
            ).astype(BF)
        return carry

    lax.fori_loop(0, NACC // 2, two_accelerations, 0)

    def out_copy(step):
        target = (q + step) % NQ
        return remote(
            outgoing.at[target], arrived.at[q], out_send.at[step - 1], out_recv.at[q],
            x * NQ + target, c,
        )

    for step in range(1, NQ):
        out_copy(step).start()
    total = outgoing[q].astype(F32)
    for step in range(1, NQ):
        source = (q + step) % NQ
        remote(
            outgoing.at[0], arrived.at[source], out_send.at[0], out_recv.at[source],
            x * NQ + source, c,
        ).wait_recv()
        total = total + arrived[source].astype(F32)
    for a in range(NACC):
        stacked[a] = total[a * TRIALS:(a + 1) * TRIALS].astype(BF)

    def sent_core(chunk, carry):
        to_core(chunk).wait_send()
        return carry

    def sent_part(n, carry):
        send_part(n).wait_send()
        return carry

    lax.fori_loop(0, PAIRS // CHUNK, sent_core, 0)
    lax.fori_loop(0, PAIRS - 1, sent_part, 0)
    for step in range(1, N_CHAN):
        delay_copy(step).wait_send()
        sub_copy(step).wait_send()
    for step in range(1, NX):
        reader_copy(step).wait_send()
        row_copy(step).wait_send()

    @pl.when(t > 0)
    def _():
        for chan in range(N_CHAN):
            halo_copy(chan).wait_send()
        for target in range(NX):
            first_copy(target).wait_send()

    for step in range(1, NQ):
        out_copy(step).wait_send()


def on_device(filterbank, channel_mask, delays, readers, stretch):
    hbm = pl.BlockSpec(memory_space=pltpu.HBM)
    vmem = pl.BlockSpec(memory_space=pltpu.VMEM)
    dma = pltpu.SemaphoreType.DMA
    return pl.pallas_call(
        kernel,
        out_shape=(
            jax.ShapeDtypeStruct((TRIALS, SHARD), BF),
            jax.ShapeDtypeStruct((NACC, TRIALS, BLK), BF),
        ),
        in_specs=[hbm] * 5,
        out_specs=(vmem, vmem),
        scratch_shapes=[
            pltpu.VMEM(filterbank.shape, BF),
            pltpu.SMEM((OWN,), jnp.int32),
            pltpu.SMEM((NACC,), F32),
            pltpu.VMEM((OWN, N_CHAN * TRIALS), jnp.int32),
            pltpu.VMEM((NACC, 1, ROWS), jnp.int32),
            pltpu.VMEM((N_CHAN, OWN, N_CHAN * TRIALS), jnp.int32),
            pltpu.SMEM((N_CHAN, OWN, N_CHAN * TRIALS), jnp.int32),
            pltpu.VMEM((NX, NACC, 1, ROWS), jnp.int32),
            pltpu.VMEM((PAIRS, ROWS, BLK), F32),
            pltpu.VMEM((PAIRS, ROWS, BLK), F32),
            pltpu.VMEM((PAIRS, ROWS, BLK), BF),
            pltpu.VMEM((PAIRS, ROWS, BLK), BF),
            pltpu.VMEM((ROWS, BLK), F32),
            pltpu.VMEM((GROUP, BLK), BF),
            pltpu.VMEM((N_CHAN, GROUP, BLK), BF),
            pltpu.VMEM((N_CHAN, OWN * GROUP, BLK), BF),
            pltpu.VMEM((2 * BLK, STEPS * BLK), BF),
            pltpu.VMEM((OWN, REACH, BLK), F32),
            pltpu.VMEM((NACC, 2 * BLK, BLK), BF),
            pltpu.VMEM((TRIALS * ROWS, BLK), F32),
            pltpu.VMEM((TRIALS * ROWS, BLK), BF),
            pltpu.VMEM((16, BLK), BF),
            pltpu.VMEM((NX, TRIALS * ROWS, BLK), BF),
            pltpu.VMEM((NX, 16, BLK), BF),
            pltpu.VMEM((TRIALS, NX, ROWS + 8, BLK), F32),
            pltpu.VMEM((NACC, 2, TRIALS * NQ, BLK), F32),
            pltpu.VMEM((NQ, NACC * TRIALS, BLK), BF),
            pltpu.VMEM((NQ, NACC * TRIALS, BLK), BF),
            dma((4,)),
            dma((N_TM,)),
            dma((PAIRS // CHUNK,)),
            dma((PAIRS // CHUNK,)),
            dma((PAIRS,)),
            dma((PAIRS,)),
        ]
        + [dma((N_CHAN,))] * 6
        + [dma]
        + [dma((NX,))] * 6
        + [dma((NQ,))] * 2,
        compiler_params=pltpu.CompilerParams(
            collective_id=0, has_side_effects=True, vmem_limit_bytes=60 * 2**20
        ),
        name="dedisperse",
    )(
        filterbank, channel_mask, delays.T, jnp.transpose(readers, (1, 2, 0)), stretch
    )


def solution(mesh):
    return jax.shard_map(
        on_device,
        mesh=mesh,
        in_specs=(
            P(("chan", "tm"), None),
            P(("chan", "tm")),
            P(None, "chan"),
            P("tm", None, None),
            P(),
        ),
        out_specs=(P("chan", "tm"), P(None, "chan", "tm")),
        check_vma=False,
    )
```

```python
import math

import jax
import jax.numpy as jnp
from jax import lax
from jax.experimental import pallas as pl
from jax.experimental.pallas import tpu as pltpu
from jax.sharding import PartitionSpec as P

MESH = pl.DeviceIdType.MESH
BF, F32 = jnp.bfloat16, jnp.float32

BLK = 128
N_TM = 64
N_CHAN = 4
SHARD = 4096
ROWS = SHARD // BLK
PAIRS = N_TM // 2
OWN = 16
TRIALS = 8
NX = 4
NQ = 16
NZ = 8
FAR_Z = (4, 3, 5, 2, 6, 1, 7, 0)
NACC = 8
GROUP = 32
LANE_GROUPS = BLK // GROUP
STACKS = OWN // LANE_GROUPS
STEPS = 4
REACH = GROUP * (STEPS + 1)
CHUNK = 4
START_OFFSET = 4.0
TAPER_HALF = 8.0


def remote(src, dst, send_sem, recv_sem, tm, chan):
    return pltpu.make_async_remote_copy(
        src_ref=src,
        dst_ref=dst,
        send_sem=send_sem,
        recv_sem=recv_sem,
        device_id=(tm, chan),
        device_id_type=MESH,
    )


def sinc_tables(stretch, table):
    row = lax.broadcasted_iota(jnp.int32, (8, BLK), 0)
    col = lax.broadcasted_iota(jnp.int32, (8, BLK), 1).astype(F32)
    factor = jnp.zeros((8, BLK), F32)
    for a in range(NACC):
        factor = jnp.where(row == a, stretch[a], factor)
    centres = START_OFFSET + col * factor
    whole = jnp.round(centres)
    odd = whole - 2.0 * jnp.floor(whole * 0.5)
    waves = (2.0 * odd - 1.0) * jnp.sin(math.pi * (centres - whole)) / math.pi
    angle = (math.pi / TAPER_HALF) * (centres - 16.0 * jnp.floor(centres / 16.0))
    cosines, sines = 0.5 * jnp.cos(angle), 0.5 * jnp.sin(angle)
    sign = (1 - 2 * (row % 2)).astype(F32)
    turns = [(math.pi / TAPER_HALF) * (row + 8 * half).astype(F32) for half in range(2)]
    turns = [(jnp.cos(angle), jnp.sin(angle)) for angle in turns]
    for a in range(NACC):
        centre, wave, cos_p, sin_p = (
            jnp.broadcast_to(part[a:a + 1], (8, BLK)) for part in (centres, waves, cosines, sines)
        )
        wave = sign * wave
        tapers = [0.5 + cos_j * cos_p + sin_j * sin_p for cos_j, sin_j in turns]
        pieces = []
        for group in range(2 * BLK // 8):
            x = (row + 8 * group).astype(F32) - centre
            sinc = jnp.where(x == 0.0, 1.0, wave / jnp.where(x == 0.0, 1.0, x))
            pieces.append(jnp.where(jnp.abs(x) < TAPER_HALF, sinc * tapers[group % 2], 0.0))
        table[a] = jnp.concatenate(pieces, axis=0).astype(BF)


def turn(blocks):
    lane_group = lax.broadcasted_iota(jnp.int32, (ROWS, BLK), 1) // GROUP
    stacked = []
    for g in range(LANE_GROUPS):
        merged = blocks[0]
        for i in range(LANE_GROUPS):
            shift = (i - g) * GROUP % BLK
            moved = pltpu.roll(blocks[i], shift, 1) if shift else blocks[i]
            merged = moved if i == 0 else jnp.where(lane_group == i, moved, merged)
        stacked.append(merged)
    return jnp.concatenate(stacked, axis=0).T


def turn_back(rows):
    lane_group = lax.broadcasted_iota(jnp.int32, (ROWS, BLK), 1) // GROUP
    flipped = rows.T
    out = []
    for i in range(LANE_GROUPS):
        merged = None
        for g in range(LANE_GROUPS):
            piece = flipped[g * ROWS:(g + 1) * ROWS]
            shift = (g - i) * GROUP % BLK
            moved = pltpu.roll(piece, shift, 1) if shift else piece
            merged = moved if g == 0 else jnp.where(lane_group == g, moved, merged)
        out.append(merged)
    return out


def lane_steps():
    shape = (2 * BLK, STEPS * BLK)
    row = lax.broadcasted_iota(jnp.int32, shape, 0)
    col = lax.broadcasted_iota(jnp.int32, shape, 1)
    group = (col % BLK) // GROUP + col // BLK + 1
    block = col % GROUP + group // LANE_GROUPS
    group = group % LANE_GROUPS
    inside = (row == group * GROUP + block) & (block < ROWS)
    beyond = (row // GROUP == LANE_GROUPS + group) & (block == ROWS)
    return jnp.where(inside | beyond, 1.0, 0.0).astype(BF)


def kernel(
    fb, mask_in, delays_in, readers_in, stretch_in,
    series_out, arrived,
    series, fb_v, mask, stretch, delays, readers_v, readers_all,
    for_core, own_sum, from_core, staged, parts,
    for_first, own_first, from_first, next_row, next_parts, halo_f,
    trials_out, trials_in, steps, reach,
    table, turned, rows, first, gathered, first_all, tall, grouped,
    outgoing, from_half, leaving,
    small_sem, result_sem, load_sem, core_send, core_recv, part_send, part_recv,
    first_core_sem, next_send, next_recv, trial_send, trial_recv,
    reader_send, reader_recv, row_send, row_recv, first_send, first_recv,
    half_send, half_recv, out_send, out_recv, own_sem,
):
    t, c = lax.axis_index("tm"), lax.axis_index("chan")
    core, me = lax.rem(t, 2), t // 2
    other = t + 1 - 2 * core
    x, q = t // NQ, lax.rem(t, NQ)
    z = q // 2

    small = [
        pltpu.make_async_copy(source, target, small_sem.at[i])
        for i, (source, target) in enumerate(
            ((mask_in, mask), (delays_in, delays), (readers_in, readers_v), (stretch_in, stretch))
        )
    ]
    for copy in small:
        copy.start()

    turn_side = 1 - 2 * core

    def chip_at(chunk, i, parity):
        half, g = chunk // 4, lax.rem(chunk, 4)
        dx = 2 - g + 3 * (g // 2) - 2 * (g // 3)
        dz = FAR_Z[i] + half * (FAR_Z[CHUNK + i] - FAR_Z[i])
        side = 1 - 2 * parity
        return NZ * lax.rem(x + NX + side * dx, NX) + lax.rem(z + NZ + side * dz, NZ)

    def load(n):
        at = pl.ds(pl.multiple_of(n * 2 * SHARD, 2 * SHARD), 2 * SHARD)
        return pltpu.make_async_copy(fb.at[:, at], fb_v.at[:, at], load_sem.at[n])

    def start_load(n, carry):
        load(n).start()
        return carry

    def greet_plane(n, carry):
        greet(lax.rem(t + n, N_TM), c)
        return carry

    def greet(tm, chan):
        pl.semaphore_signal(barrier, inc=1, device_id=(tm, chan), device_id_type=MESH)

    barrier = pltpu.get_barrier_semaphore()
    lax.fori_loop(0, 8, start_load, 0)
    lax.fori_loop(24, 48, greet_plane, 0)
    lax.fori_loop(8, PAIRS, start_load, 0)
    lax.fori_loop(1, 24, greet_plane, 0)
    lax.fori_loop(48, N_TM, greet_plane, 0)
    for step in range(1, N_CHAN):
        greet(t, lax.rem(c + step, N_CHAN))

    for copy in small:
        copy.wait()
    sublane = lax.broadcasted_iota(jnp.int32, (8, BLK), 0)
    weights = []
    for half in range(2):
        value = jnp.zeros((8, BLK), F32)
        for i in range(8):
            value = jnp.where(sublane == i, mask[8 * half + i].astype(F32), value)
        weights.append(value)

    def block_sum(at):
        block = fb_v[:, pl.ds(at, BLK)].astype(F32)
        return block[:8] * weights[0] + block[8:] * weights[1]

    def merge(blocks):
        step = 1
        while len(blocks) > 1:
            even = (sublane // step) % 2 == 0
            blocks = [
                jnp.where(even, a, b) + pltpu.roll(jnp.where(even, b, a), 8 - step, 0)
                for a, b in zip(blocks[0::2], blocks[1::2])
            ]
            step *= 2
        return blocks[0]

    def shard_sum(shard):
        base = pl.multiple_of(shard * SHARD, SHARD)
        return jnp.concatenate(
            [
                merge([block_sum(base + (8 * group + i) * BLK) for i in range(8)])
                for group in range(ROWS // 8)
            ],
            axis=0,
        )

    to_core = remote(for_core, from_core, core_send, core_recv, other, c)

    def sum_chip(n, carry):
        load(n).wait()
        for_core[n] = shard_sum(2 * n + 1 - core)
        own_sum[n] = shard_sum(2 * n + core)
        for_first[pl.ds(n, 1)] = for_core[n, :1]
        own_first[pl.ds(n, 1)] = own_sum[n, :1]
        return carry

    lax.fori_loop(0, PAIRS, sum_chip, 0)
    pl.semaphore_wait(barrier, N_TM - 1 + N_CHAN - 1)

    first_to_core = remote(
        own_first, from_first, first_core_sem.at[0], first_core_sem.at[1], other, c
    )

    to_core.start()
    first_to_core.start()

    def reader_copy(step):
        return remote(
            readers_v, readers_all.at[x], reader_send.at[step - 1], reader_recv.at[x],
            lax.rem(x + step, NX) * NQ + q, c,
        )

    for step in range(1, NX):
        reader_copy(step).start()
    readers_all[x] = readers_v[...]

    def send_part(chunk, i):
        chip = chip_at(chunk, i, core)
        return remote(
            staged.at[chip], parts.at[me], part_send, part_recv,
            2 * chip + core, c,
        )

    to_core.wait_recv()

    def send_parts(chunk, carry):
        for i in range(CHUNK):
            chip = chip_at(chunk, i, core)
            staged[chip] = (own_sum[chip] + from_core[chip]).astype(BF)
            if i < CHUNK - 1:
                send_part(chunk, i).start()
            else:
                @pl.when(chunk < PAIRS // CHUNK - 1)
                def _():
                    send_part(chunk, i).start()

        return carry

    def send_next(chunk, i):
        chip = chip_at(chunk, i, core)
        return remote(
            next_row.at[chip + core], next_parts.at[me], next_send, next_recv,
            2 * chip + core, c,
        )

    def send_nexts(chunk, carry):
        for i in range(CHUNK):
            if i < CHUNK - 1:
                send_next(chunk, i).start()
            else:
                @pl.when(chunk < PAIRS // CHUNK - 1)
                def _():
                    send_next(chunk, i).start()

        return carry

    lax.fori_loop(0, PAIRS // CHUNK, send_parts, 0)
    first_to_core.wait_recv()
    next_row[PAIRS:] = jnp.zeros((1, 1, BLK), F32)
    next_row[:PAIRS] = (for_first[...] + from_first[...]).reshape(PAIRS, 1, BLK)
    lax.fori_loop(0, PAIRS // CHUNK, send_nexts, 0)
    parts[me] = staged[me]
    next_parts[me] = next_row[me + core]

    sinc_tables(stretch, table)
    steps[...] = lane_steps()
    halo_f[...] = jnp.zeros_like(halo_f)
    for step in range(1, NX):
        source = lax.rem(x + step, NX)
        remote(
            readers_v, readers_all.at[source], reader_send.at[0], reader_recv.at[source],
            source * NQ + q, c,
        ).wait_recv()
    names = jnp.concatenate([readers_all[source][:, 0, :] for source in range(NX)], axis=1)
    reader_row = lax.broadcasted_iota(jnp.int32, (NQ, BLK), 0) + x * NQ
    pick = jnp.concatenate(
        [(names[a:a + 1] == reader_row).astype(F32) for a in range(NACC)], axis=0
    ).astype(BF)

    others = pl.ds(0, PAIRS - 1)
    all_parts = remote(parts.at[others], parts.at[others], part_send, part_recv, other, c)
    all_nexts = remote(
        next_parts.at[others], next_parts.at[others], next_send, next_recv, other, c
    )
    all_parts.wait_recv()
    own = []
    for stack in range(STACKS):
        blocks = []
        for k in range(stack * LANE_GROUPS, (stack + 1) * LANE_GROUPS):
            blocks.append(parts[2 * k].astype(F32) + parts[2 * k + 1].astype(F32))
        own.append(turn(blocks).astype(BF))
    own = jnp.concatenate(own, axis=0)
    reach[:, :GROUP] = own.astype(F32).reshape(OWN, GROUP, BLK)

    all_nexts.wait_recv()
    for k in range(OWN):
        halo_f[k:k + 1] = next_parts[2 * k] + next_parts[2 * k + 1]
    first_blocks = halo_f[...]
    beyond = jnp.concatenate(
        [first_blocks] + [pltpu.roll(first_blocks, BLK - g * GROUP, 1) for g in range(1, LANE_GROUPS)],
        axis=0,
    ).T[:GROUP]
    lane = lax.broadcasted_iota(jnp.int32, (GROUP, BLK), 1)
    next_blocks = jnp.concatenate(
        [jnp.where(lane % GROUP == k, beyond, 0.0).astype(BF) for k in range(OWN)], axis=0
    )
    both = jnp.concatenate([own, next_blocks], axis=1)
    for pair in range(STEPS // 2):
        moved = jnp.dot(
            both, steps[:, pair * 2 * BLK:(pair + 1) * 2 * BLK], preferred_element_type=F32
        )
        for i in range(2):
            e = 2 * pair + i + 1
            reach[:, e * GROUP:(e + 1) * GROUP] = moved[:, i * BLK:(i + 1) * BLK].reshape(
                OWN, GROUP, BLK
            )

    def trials_of(chan):
        def one_band(k, sums):
            return tuple(
                sums[m] + reach[k, pl.ds(delays[k, chan * TRIALS + m], GROUP)]
                for m in range(TRIALS)
            )

        return lax.fori_loop(
            0, OWN, one_band, tuple(jnp.zeros((GROUP, BLK), F32) for _ in range(TRIALS))
        )

    def chan_at(step):
        return lax.rem(c + N_CHAN + turn_side * step, N_CHAN)

    def trial_copy(step):
        return remote(
            trials_out.at[step - 1], trials_in.at[c], trial_send.at[step - 1], trial_recv.at[c],
            t, chan_at(step),
        )

    for step in (2, 1, 3):
        sums = trials_of(chan_at(step))
        trials_out[step - 1] = jnp.concatenate(sums, axis=0).astype(BF)
        trial_copy(step).start()
    totals = jnp.concatenate(trials_of(c), axis=0)
    to_core.wait_send()
    first_to_core.wait_send()
    all_parts.wait_send()
    all_nexts.wait_send()
    for step in range(1, NX):
        reader_copy(step).wait_send()
    for step in (1, 3, 2):
        source = chan_at(step)
        remote(
            trials_out.at[0], trials_in.at[source], trial_send.at[0], trial_recv.at[source],
            t, source,
        ).wait_recv()
        totals = totals + trials_in[source].astype(F32)

    def row_copy(half, step):
        return remote(
            rows.at[half], gathered.at[x, half], row_send.at[half, step - 1], row_recv.at[half, x],
            lax.rem(x + NX + turn_side * step, NX) * NQ + q, c,
        )

    def first_copy(target):
        return remote(
            first, first_all.at[(t - 1) // NQ], first_send.at[target],
            first_recv.at[(t - 1) // NQ], target * NQ + lax.rem(t - 1, NQ), c,
        )

    backs = []
    for pair in range(TRIALS // LANE_GROUPS):
        backs += turn_back(totals[pair * BLK:(pair + 1) * BLK])
    first[...] = jnp.concatenate(
        [back[:1] for back in backs] + [jnp.zeros((TRIALS, BLK), F32)], axis=0
    ).astype(BF)

    @pl.when(t > 0)
    def _():
        for target in range(NX):
            first_copy(target).start()

    for half in range(2):
        for i in range(LANE_GROUPS):
            rows[half, i * ROWS:(i + 1) * ROWS] = backs[half * LANE_GROUPS + i].astype(BF)
        for step in (2, 1, 3):
            row_copy(half, step).start()
    gathered[x] = rows[...]
    for m in range(TRIALS):
        turned[pl.ds(m, ROWS, stride=TRIALS)] = backs[m]
    for b in range(ROWS):
        series[:, b * BLK:(b + 1) * BLK] = turned[b * TRIALS:(b + 1) * TRIALS].astype(BF)

    series_copy = pltpu.make_async_copy(series, series_out, result_sem)
    series_copy.start()

    for step in range(1, N_CHAN):
        trial_copy(step).wait_send()

    def first_arrival(source):
        return remote(
            first, first_all.at[source], first_send.at[0], first_recv.at[source],
            source * NQ + q + 1, c,
        )

    for step in (0, 1, 3, 2):
        source = lax.rem(x + step, NX)
        if step:
            for half in range(2):
                remote(
                    rows.at[half], gathered.at[source, half], row_send.at[half, 0],
                    row_recv.at[half, source], source * NQ + q, c,
                ).wait_recv()
        for m in range(TRIALS):
            at = m % LANE_GROUPS * ROWS
            tall[m, source, :ROWS] = gathered[source, m // LANE_GROUPS, at:at + ROWS].astype(F32)
    for step in (0, 1, 3, 2):
        source = lax.rem(x + step, NX)
        last_block = source * NQ + q == N_TM - 1

        @pl.when(jnp.logical_not(last_block))
        def _():
            first_arrival(source).wait_recv()

        @pl.when(last_block)
        def _():
            first_all[NX - 1] = jnp.zeros((16, BLK), BF)

        last = first_all[source].astype(F32)
        for m in range(TRIALS):
            tall[m, source, ROWS:ROWS + 1] = last[m:m + 1]

    for m in range(TRIALS):
        for half in range(2):
            block = jnp.concatenate(
                [tall[m, source, half:half + ROWS] for source in range(NX)], axis=0
            ).astype(BF)
            sums = jnp.dot(pick, block, preferred_element_type=F32)
            for a in range(NACC):
                grouped[a, half, pl.ds(m, NQ, stride=TRIALS)] = sums[a * NQ:(a + 1) * NQ]

    def half_copy(half):
        return remote(
            outgoing.at[1 - core, half], from_half.at[half], half_send.at[half], half_recv.at[half],
            other, c,
        )

    def z_at(n):
        return lax.rem(z + NZ + turn_side * FAR_Z[n], NZ)

    def out_copy(half, n):
        target = z_at(n)
        return remote(
            leaving.at[half, target], arrived.at[half, z],
            out_send.at[half], out_recv.at[half], x * NQ + 2 * target + core, c,
        )

    def sent_out(half):
        others = pl.ds(0, NZ - 1)
        return remote(
            leaving.at[half, others], arrived.at[half, others],
            out_send.at[half], out_recv.at[half], other, c,
        )

    def own_copy(half):
        return pltpu.make_async_copy(
            leaving.at[half, z], arrived.at[half, z], own_sem.at[half]
        )

    for half in range(2):
        for pair in range(2):
            results = []
            for i in range(2):
                a = 4 * half + 2 * pair + i
                block = jnp.concatenate([grouped[a, 0], grouped[a, 1]], axis=1).astype(BF)
                results.append(jnp.dot(block, table[a], preferred_element_type=F32))
            for reader in range(NQ):
                at = slice(reader * TRIALS, (reader + 1) * TRIALS)
                outgoing[reader % 2, half, reader // 2, pair * 16:(pair + 1) * 16] = (
                    jnp.concatenate([results[0][at], results[1][at]], axis=0)
                )
        half_copy(half).start()
    for half in range(2):
        half_copy(half).wait_recv()
        for n in range(NZ):
            target = z_at(n)
            leaving[half, target] = (outgoing[core, half, target] + from_half[half, target]).astype(BF)
            if n < NZ - 1:
                out_copy(half, n).start()
            else:
                own_copy(half).start()
    for step in range(1, NX):
        for half in range(2):
            row_copy(half, step).wait_send()

    @pl.when(t > 0)
    def _():
        for target in range(NX):
            first_copy(target).wait_send()

    for half in range(2):
        half_copy(half).wait_send()
    series_copy.wait()
    for half in range(2):
        sent_out(half).wait_recv()

    for half in range(2):
        sent_out(half).wait_send()
        own_copy(half).wait()


def finish(series_in, arrived, series, stacked):
    series[...] = series_in[...]
    for half in range(2):
        total = arrived[half, 0].astype(F32)
        for source in range(1, NZ):
            total = total + arrived[half, source].astype(F32)
        for i in range(NACC // 2):
            stacked[half * (NACC // 2) + i] = total[i * TRIALS:(i + 1) * TRIALS].astype(BF)


def on_device(filterbank, channel_mask, delays, readers, stretch):
    hbm = pl.BlockSpec(memory_space=pltpu.HBM)
    vmem = pl.BlockSpec(memory_space=pltpu.VMEM)
    dma = pltpu.SemaphoreType.DMA
    results = pl.pallas_call(
        kernel,
        out_shape=(
            jax.ShapeDtypeStruct((TRIALS, SHARD), BF),
            jax.ShapeDtypeStruct((2, NZ, NACC * TRIALS // 2, BLK), BF),
        ),
        in_specs=[hbm] * 5,
        out_specs=(hbm, hbm),
        scratch_shapes=[
            pltpu.VMEM((TRIALS, SHARD), BF),
            pltpu.VMEM(filterbank.shape, BF),
            pltpu.SMEM((OWN,), jnp.int32),
            pltpu.SMEM((NACC,), F32),
            pltpu.SMEM((OWN, N_CHAN * TRIALS), jnp.int32),
            pltpu.VMEM((NACC, 1, ROWS), jnp.int32),
            pltpu.VMEM((NX, NACC, 1, ROWS), jnp.int32),
            pltpu.VMEM((PAIRS, ROWS, BLK), F32),
            pltpu.VMEM((PAIRS, ROWS, BLK), F32),
            pltpu.VMEM((PAIRS, ROWS, BLK), F32),
            pltpu.VMEM((PAIRS, ROWS, BLK), BF),
            pltpu.VMEM((PAIRS, ROWS, BLK), BF),
            pltpu.VMEM((PAIRS, BLK), F32),
            pltpu.VMEM((PAIRS, BLK), F32),
            pltpu.VMEM((PAIRS, BLK), F32),
            pltpu.VMEM((PAIRS + 1, 1, BLK), F32),
            pltpu.VMEM((PAIRS, 1, BLK), F32),
            pltpu.VMEM((ROWS, BLK), F32),
            pltpu.VMEM((N_CHAN - 1, TRIALS * GROUP, BLK), BF),
            pltpu.VMEM((N_CHAN, TRIALS * GROUP, BLK), BF),
            pltpu.VMEM((2 * BLK, STEPS * BLK), BF),
            pltpu.VMEM((OWN, REACH, BLK), F32),
            pltpu.VMEM((NACC, 2 * BLK, BLK), BF),
            pltpu.VMEM((TRIALS * ROWS, BLK), F32),
            pltpu.VMEM((2, BLK, BLK), BF),
            pltpu.VMEM((16, BLK), BF),
            pltpu.VMEM((NX, 2, BLK, BLK), BF),
            pltpu.VMEM((NX, 16, BLK), BF),
            pltpu.VMEM((TRIALS, NX, ROWS + 8, BLK), F32),
            pltpu.VMEM((NACC, 2, TRIALS * NQ, BLK), F32),
            pltpu.VMEM((2, 2, NZ, NACC * TRIALS // 2, BLK), F32),
            pltpu.VMEM((2, NZ, NACC * TRIALS // 2, BLK), F32),
            pltpu.VMEM((2, NZ, NACC * TRIALS // 2, BLK), BF),
            dma((4,)),
            dma,
            dma((PAIRS,)),
            dma,
            dma,
            dma,
            dma,
            dma((2,)),
            dma,
            dma,
            dma((N_CHAN,)),
            dma((N_CHAN,)),
            dma((NX,)),
            dma((NX,)),
            dma((2, NX)),
            dma((2, NX)),
            dma((NX,)),
            dma((NX,)),
            dma((2,)),
            dma((2,)),
            dma((2,)),
            dma((2,)),
            dma((2,)),
        ],
        compiler_params=pltpu.CompilerParams(
            collective_id=0, has_side_effects=True, vmem_limit_bytes=60 * 2**20
        ),
        name="dedisperse",
    )(
        filterbank, channel_mask, delays.T, jnp.transpose(readers, (1, 2, 0)), stretch
    )
    return pl.pallas_call(
        finish,
        out_shape=(
            jax.ShapeDtypeStruct((TRIALS, SHARD), BF),
            jax.ShapeDtypeStruct((NACC, TRIALS, BLK), BF),
        ),
        in_specs=[vmem] * 2,
        out_specs=(vmem, vmem),
        compiler_params=pltpu.CompilerParams(vmem_limit_bytes=60 * 2**20),
        name="results",
    )(*results)


def solution(mesh):
    return jax.shard_map(
        on_device,
        mesh=mesh,
        in_specs=(
            P(("chan", "tm"), None),
            P(("chan", "tm")),
            P(None, "chan"),
            P("tm", None, None),
            P(),
        ),
        out_specs=(P("chan", "tm"), P(None, "chan", "tm")),
        check_vma=False,
    )
```

```python
import math

import jax
import jax.numpy as jnp
from jax import lax
from jax.experimental import pallas as pl
from jax.experimental.pallas import tpu as pltpu
from jax.sharding import PartitionSpec as P

MESH = pl.DeviceIdType.MESH
BF, F32 = jnp.bfloat16, jnp.float32

BLK = 128
N_TM = 64
N_CHAN = 4
SHARD = 4096
ROWS = SHARD // BLK
PAIRS = N_TM // 2
OWN = 16
TRIALS = 8
HALF = TRIALS // 2
NX = 4
NQ = 16
NZ = 8
FAR_X = (2, 1, 3, 0)
FAR_Z = (4, 3, 5, 2, 6, 1, 7, 0)
NACC = 8
GROUP = 32
LANE_GROUPS = BLK // GROUP
STACKS = OWN // LANE_GROUPS
STEPS = 4
REACH = GROUP * (STEPS + 1)
CHUNK = 4
START_OFFSET = 4.0
TAPER_HALF = 8.0


def remote(src, dst, send_sem, recv_sem, tm, chan):
    return pltpu.make_async_remote_copy(
        src_ref=src,
        dst_ref=dst,
        send_sem=send_sem,
        recv_sem=recv_sem,
        device_id=(tm, chan),
        device_id_type=MESH,
    )


def sinc_tables(stretch, table):
    row = lax.broadcasted_iota(jnp.int32, (8, BLK), 0)
    col = lax.broadcasted_iota(jnp.int32, (8, BLK), 1).astype(F32)
    factor = jnp.zeros((8, BLK), F32)
    for a in range(NACC):
        factor = jnp.where(row == a, stretch[a], factor)
    centres = START_OFFSET + col * factor
    whole = jnp.round(centres)
    odd = whole - 2.0 * jnp.floor(whole * 0.5)
    waves = (2.0 * odd - 1.0) * jnp.sin(math.pi * (centres - whole)) / math.pi
    angle = (math.pi / TAPER_HALF) * (centres - 16.0 * jnp.floor(centres / 16.0))
    cosines, sines = 0.5 * jnp.cos(angle), 0.5 * jnp.sin(angle)
    sign = (1 - 2 * (row % 2)).astype(F32)
    turns = [(math.pi / TAPER_HALF) * (row + 8 * half).astype(F32) for half in range(2)]
    turns = [(jnp.cos(angle), jnp.sin(angle)) for angle in turns]
    for a in range(NACC):
        centre, wave, cos_p, sin_p = (
            jnp.broadcast_to(part[a:a + 1], (8, BLK)) for part in (centres, waves, cosines, sines)
        )
        wave = sign * wave
        tapers = [0.5 + cos_j * cos_p + sin_j * sin_p for cos_j, sin_j in turns]
        pieces = []
        for group in range(2 * BLK // 8):
            x = (row + 8 * group).astype(F32) - centre
            sinc = jnp.where(x == 0.0, 1.0, wave / jnp.where(x == 0.0, 1.0, x))
            pieces.append(jnp.where(jnp.abs(x) < TAPER_HALF, sinc * tapers[group % 2], 0.0))
        table[a] = jnp.concatenate(pieces, axis=0).astype(BF)


def turn(blocks):
    lane_group = lax.broadcasted_iota(jnp.int32, (ROWS, BLK), 1) // GROUP
    stacked = []
    for g in range(LANE_GROUPS):
        merged = blocks[0]
        for i in range(LANE_GROUPS):
            shift = (i - g) * GROUP % BLK
            moved = pltpu.roll(blocks[i], shift, 1) if shift else blocks[i]
            merged = moved if i == 0 else jnp.where(lane_group == i, moved, merged)
        stacked.append(merged)
    return jnp.concatenate(stacked, axis=0).T


def turn_back(rows):
    lane_group = lax.broadcasted_iota(jnp.int32, (ROWS, BLK), 1) // GROUP
    flipped = rows.T
    out = []
    for i in range(LANE_GROUPS):
        merged = None
        for g in range(LANE_GROUPS):
            piece = flipped[g * ROWS:(g + 1) * ROWS]
            shift = (g - i) * GROUP % BLK
            moved = pltpu.roll(piece, shift, 1) if shift else piece
            merged = moved if g == 0 else jnp.where(lane_group == g, moved, merged)
        out.append(merged)
    return out


def lane_steps():
    shape = (2 * BLK, STEPS * BLK)
    row = lax.broadcasted_iota(jnp.int32, shape, 0)
    col = lax.broadcasted_iota(jnp.int32, shape, 1)
    group = (col % BLK) // GROUP + col // BLK + 1
    block = col % GROUP + group // LANE_GROUPS
    group = group % LANE_GROUPS
    inside = (row == group * GROUP + block) & (block < ROWS)
    beyond = (row // GROUP == LANE_GROUPS + group) & (block == ROWS)
    return jnp.where(inside | beyond, 1.0, 0.0).astype(BF)


def kernel(
    fb, mask_in, delays_in, readers_in, stretch_in,
    series_out, arrived,
    series, fb_v, mask, stretch, delays, readers_v, readers_all,
    for_core, own_sum, from_core, staged, parts,
    for_first, own_first, from_first, next_row, next_parts, halo_f,
    trials_out, trials_in, steps, reach,
    table, turned, rows, first, gathered, first_all, tall, grouped,
    outgoing, from_half, leaving,
    small_sem, result_sem, load_sem, core_send, core_recv, part_send, part_recv,
    first_core_sem, next_send, next_recv, trial_send, trial_recv,
    reader_send, reader_recv, row_send, row_recv, first_send, first_recv,
    half_send, half_recv, out_send, out_recv, own_sem,
):
    t, c = lax.axis_index("tm"), lax.axis_index("chan")
    core, me = lax.rem(t, 2), t // 2
    other = t + 1 - 2 * core
    x, q = t // NQ, lax.rem(t, NQ)
    z = q // 2

    small = [
        pltpu.make_async_copy(source, target, small_sem.at[i])
        for i, (source, target) in enumerate(
            ((mask_in, mask), (delays_in, delays), (readers_in, readers_v), (stretch_in, stretch))
        )
    ]
    for copy in small:
        copy.start()

    turn_side = 1 - 2 * core

    def chip_at(chunk, i, parity):
        if isinstance(chunk, int):
            half, dx = chunk // 4, FAR_X[chunk % 4]
        else:
            half, g = chunk // 4, lax.rem(chunk, 4)
            dx = 2 - g + 3 * (g // 2) - 2 * (g // 3)
        dz = FAR_Z[i] + half * (FAR_Z[CHUNK + i] - FAR_Z[i])
        side = 1 - 2 * parity
        return NZ * lax.rem(x + NX + side * dx, NX) + lax.rem(z + NZ + side * dz, NZ)

    def load(n):
        at = pl.ds(pl.multiple_of(n * 2 * SHARD, 2 * SHARD), 2 * SHARD)
        return pltpu.make_async_copy(fb.at[:, at], fb_v.at[:, at], load_sem.at[n])

    def start_load(n, carry):
        load(n).start()
        return carry

    def greet_plane(n, carry):
        greet(lax.rem(t + n, N_TM), c)
        return carry

    def greet(tm, chan):
        pl.semaphore_signal(barrier, inc=1, device_id=(tm, chan), device_id_type=MESH)

    barrier = pltpu.get_barrier_semaphore()
    lax.fori_loop(0, 8, start_load, 0)
    lax.fori_loop(24, 48, greet_plane, 0)
    lax.fori_loop(8, PAIRS, start_load, 0)
    lax.fori_loop(1, 24, greet_plane, 0)
    lax.fori_loop(48, N_TM, greet_plane, 0)
    for step in range(1, N_CHAN):
        greet(t, lax.rem(c + step, N_CHAN))

    for copy in small:
        copy.wait()
    sublane = lax.broadcasted_iota(jnp.int32, (8, BLK), 0)
    weights = []
    for half in range(2):
        value = jnp.zeros((8, BLK), F32)
        for i in range(8):
            value = jnp.where(sublane == i, mask[8 * half + i].astype(F32), value)
        weights.append(value)

    def block_sum(at):
        block = fb_v[:, pl.ds(at, BLK)].astype(F32)
        return block[:8] * weights[0] + block[8:] * weights[1]

    def merge(blocks):
        step = 1
        while len(blocks) > 1:
            even = (sublane // step) % 2 == 0
            blocks = [
                jnp.where(even, a, b) + pltpu.roll(jnp.where(even, b, a), 8 - step, 0)
                for a, b in zip(blocks[0::2], blocks[1::2])
            ]
            step *= 2
        return blocks[0]

    def shard_sum(shard):
        base = pl.multiple_of(shard * SHARD, SHARD)
        return jnp.concatenate(
            [
                merge([block_sum(base + (8 * group + i) * BLK) for i in range(8)])
                for group in range(ROWS // 8)
            ],
            axis=0,
        )

    def to_core(row):
        at = pl.ds(pl.multiple_of(row * NZ, NZ), NZ)
        return remote(
            for_core.at[at], from_core.at[at], core_send.at[row], core_recv.at[row], other, c
        )


    def sum_chip(n, carry):
        load(n).wait()
        for_core[n] = shard_sum(2 * n + 1 - core)
        own_sum[n] = shard_sum(2 * n + core)
        for_first[pl.ds(n, 1)] = for_core[n, :1]
        own_first[pl.ds(n, 1)] = own_sum[n, :1]
        return carry

    lax.fori_loop(0, PAIRS, sum_chip, 0)
    pl.semaphore_wait(barrier, N_TM - 1 + N_CHAN - 1)

    first_to_core = remote(
        own_first, from_first, first_core_sem.at[0], first_core_sem.at[1], other, c
    )

    first_to_core.start()
    for g in range(NX):
        to_core(lax.rem(x + NX - turn_side * FAR_X[g], NX)).start()

    def reader_copy(step):
        return remote(
            readers_v, readers_all.at[x], reader_send.at[step - 1], reader_recv.at[x],
            lax.rem(x + step, NX) * NQ + q, c,
        )

    for step in range(1, NX):
        reader_copy(step).start()
    readers_all[x] = readers_v[...]

    def send_part(chunk, i):
        chip = chip_at(chunk, i, core)
        return remote(
            staged.at[chip], parts.at[me], part_send, part_recv,
            2 * chip + core, c,
        )

    def send_parts(chunk, carry):
        for i in range(CHUNK):
            chip = chip_at(chunk, i, core)
            staged[chip] = (own_sum[chip] + from_core[chip]).astype(BF)
            if i < CHUNK - 1 or isinstance(chunk, int):
                send_part(chunk, i).start()
                send_next(chunk, i).start()
            else:
                @pl.when(chunk < PAIRS // CHUNK - 1)
                def _():
                    send_part(chunk, i).start()
                    send_next(chunk, i).start()

        return carry

    def send_next(chunk, i):
        chip = chip_at(chunk, i, core)
        return remote(
            next_row.at[chip + core], next_parts.at[me], next_send, next_recv,
            2 * chip + core, c,
        )

    first_to_core.wait_recv()
    next_row[PAIRS:] = jnp.zeros((1, 1, BLK), F32)
    next_row[:PAIRS] = (for_first[...] + from_first[...]).reshape(PAIRS, 1, BLK)

    for chunk in range(NX):
        to_core(lax.rem(x + NX + turn_side * FAR_X[chunk], NX)).wait_recv()
        send_parts(chunk, 0)
    lax.fori_loop(NX, PAIRS // CHUNK, send_parts, 0)
    parts[me] = staged[me]
    next_parts[me] = next_row[me + core]

    sinc_tables(stretch, table)
    steps[...] = lane_steps()
    halo_f[...] = jnp.zeros_like(halo_f)
    for step in range(1, NX):
        source = lax.rem(x + step, NX)
        remote(
            readers_v, readers_all.at[source], reader_send.at[0], reader_recv.at[source],
            source * NQ + q, c,
        ).wait_recv()
    names = jnp.concatenate([readers_all[source][:, 0, :] for source in range(NX)], axis=1)
    reader_row = lax.broadcasted_iota(jnp.int32, (NQ, BLK), 0) + x * NQ
    pick = jnp.concatenate(
        [(names[a:a + 1] == reader_row).astype(F32) for a in range(NACC)], axis=0
    ).astype(BF)

    others = pl.ds(0, PAIRS - 1)
    all_parts = remote(parts.at[others], parts.at[others], part_send, part_recv, other, c)
    all_nexts = remote(
        next_parts.at[others], next_parts.at[others], next_send, next_recv, other, c
    )
    all_parts.wait_recv()
    own = []
    for stack in range(STACKS):
        blocks = []
        for k in range(stack * LANE_GROUPS, (stack + 1) * LANE_GROUPS):
            blocks.append(parts[2 * k].astype(F32) + parts[2 * k + 1].astype(F32))
        own.append(turn(blocks).astype(BF))
    own = jnp.concatenate(own, axis=0)
    reach[:, :GROUP] = own.astype(F32).reshape(OWN, GROUP, BLK)

    all_nexts.wait_recv()
    for k in range(OWN):
        halo_f[k:k + 1] = next_parts[2 * k] + next_parts[2 * k + 1]
    first_blocks = halo_f[...]
    beyond = jnp.concatenate(
        [first_blocks] + [pltpu.roll(first_blocks, BLK - g * GROUP, 1) for g in range(1, LANE_GROUPS)],
        axis=0,
    ).T[:GROUP]
    lane = lax.broadcasted_iota(jnp.int32, (GROUP, BLK), 1)
    next_blocks = jnp.concatenate(
        [jnp.where(lane % GROUP == k, beyond, 0.0).astype(BF) for k in range(OWN)], axis=0
    )
    both = jnp.concatenate([own, next_blocks], axis=1)
    for pair in range(STEPS // 2):
        moved = jnp.dot(
            both, steps[:, pair * 2 * BLK:(pair + 1) * 2 * BLK], preferred_element_type=F32
        )
        for i in range(2):
            e = 2 * pair + i + 1
            reach[:, e * GROUP:(e + 1) * GROUP] = moved[:, i * BLK:(i + 1) * BLK].reshape(
                OWN, GROUP, BLK
            )

    def trials_of(chan, half):
        def one_band(k, sums):
            return tuple(
                sums[m] + reach[k, pl.ds(delays[k, chan * TRIALS + half * HALF + m], GROUP)]
                for m in range(HALF)
            )

        sums = tuple(jnp.zeros((GROUP, BLK), F32) for _ in range(HALF))
        return jnp.concatenate(lax.fori_loop(0, OWN, one_band, sums, unroll=2), axis=0)

    def chan_at(step):
        return lax.rem(c + N_CHAN + turn_side * step, N_CHAN)

    def trial_copy(half, step):
        return remote(
            trials_out.at[half, step - 1], trials_in.at[half, c],
            trial_send.at[half, step - 1], trial_recv.at[half, c], t, chan_at(step),
        )

    for half in range(2):
        for step in (2, 1, 3):
            trials_out[half, step - 1] = trials_of(chan_at(step), half).astype(BF)
            trial_copy(half, step).start()
    totals = [trials_of(c, half) for half in range(2)]
    for row in range(NX):
        to_core(row).wait_send()
    first_to_core.wait_send()
    all_parts.wait_send()
    all_nexts.wait_send()
    for step in range(1, NX):
        reader_copy(step).wait_send()

    def row_copy(half, step):
        return remote(
            rows.at[half], gathered.at[x, half], row_send.at[half, step - 1], row_recv.at[half, x],
            lax.rem(x + NX + turn_side * step, NX) * NQ + q, c,
        )

    def first_copy(target):
        return remote(
            first, first_all.at[(t - 1) // NQ], first_send.at[target],
            first_recv.at[(t - 1) // NQ], target * NQ + lax.rem(t - 1, NQ), c,
        )

    backs = []
    for half in range(2):
        total = totals[half]
        for step in (1, 3, 2):
            source = chan_at(step)
            remote(
                trials_out.at[half, 0], trials_in.at[half, source],
                trial_send.at[half, 0], trial_recv.at[half, source], t, source,
            ).wait_recv()
            total = total + trials_in[half, source].astype(F32)
        backs += turn_back(total)
        if half == 1:
            first[...] = jnp.concatenate(
                [back[:1] for back in backs] + [jnp.zeros((TRIALS, BLK), F32)], axis=0
            ).astype(BF)

            @pl.when(t > 0)
            def _():
                for target in range(NX):
                    first_copy(target).start()

        for i in range(HALF):
            rows[half, i * ROWS:(i + 1) * ROWS] = backs[half * HALF + i].astype(BF)
        for step in (2, 1, 3):
            row_copy(half, step).start()
    gathered[x] = rows[...]
    for m in range(TRIALS):
        turned[pl.ds(m, ROWS, stride=TRIALS)] = backs[m]
    for b in range(ROWS):
        series[:, b * BLK:(b + 1) * BLK] = turned[b * TRIALS:(b + 1) * TRIALS].astype(BF)

    series_copy = pltpu.make_async_copy(series, series_out, result_sem)
    series_copy.start()

    for half in range(2):
        for step in range(1, N_CHAN):
            trial_copy(half, step).wait_send()

    def first_arrival(source):
        return remote(
            first, first_all.at[source], first_send.at[0], first_recv.at[source],
            source * NQ + q + 1, c,
        )

    def group(m, upper, block):
        sums = jnp.dot(pick, block, preferred_element_type=F32)
        for a in range(NACC):
            grouped[a, upper, pl.ds(m, NQ, stride=TRIALS)] = sums[a * NQ:(a + 1) * NQ]

    for half in range(2):
        for step in (1, 3, 2):
            source = lax.rem(x + step, NX)
            remote(
                rows.at[half], gathered.at[source, half], row_send.at[half, 0],
                row_recv.at[half, source], source * NQ + q, c,
            ).wait_recv()
        for i in range(HALF):
            m, at = half * HALF + i, i * ROWS
            pieces = [gathered[source, half, at:at + ROWS] for source in range(NX)]
            group(m, 0, jnp.concatenate(pieces, axis=0))
            for source in range(NX):
                tall[m, source, :ROWS] = pieces[source].astype(F32)
    for source in range(NX):
        last_block = source * NQ + q == N_TM - 1

        @pl.when(jnp.logical_not(last_block))
        def _():
            first_arrival(source).wait_recv()

        @pl.when(last_block)
        def _():
            first_all[source] = jnp.zeros((16, BLK), BF)

        last = first_all[source].astype(F32)
        for m in range(TRIALS):
            tall[m, source, ROWS:ROWS + 1] = last[m:m + 1]
    for m in range(TRIALS):
        group(
            m, 1,
            jnp.concatenate([tall[m, source, 1:1 + ROWS] for source in range(NX)], axis=0).astype(BF),
        )

    def half_copy(half):
        return remote(
            outgoing.at[1 - core, half], from_half.at[half], half_send.at[half], half_recv.at[half],
            other, c,
        )

    def z_at(n):
        return lax.rem(z + NZ + turn_side * FAR_Z[n], NZ)

    def out_copy(half, n):
        target = z_at(n)
        return remote(
            leaving.at[half, target], arrived.at[half, z],
            out_send.at[half], out_recv.at[half], x * NQ + 2 * target + core, c,
        )

    def sent_out(half):
        others = pl.ds(0, NZ - 1)
        return remote(
            leaving.at[half, others], arrived.at[half, others],
            out_send.at[half], out_recv.at[half], other, c,
        )

    def own_copy(half):
        return pltpu.make_async_copy(
            leaving.at[half, z], arrived.at[half, z], own_sem.at[half]
        )

    for half in range(2):
        for pair in range(2):
            results = []
            for i in range(2):
                a = 4 * half + 2 * pair + i
                block = jnp.concatenate([grouped[a, 0], grouped[a, 1]], axis=1).astype(BF)
                results.append(jnp.dot(block, table[a], preferred_element_type=F32))
            for reader in range(NQ):
                at = slice(reader * TRIALS, (reader + 1) * TRIALS)
                outgoing[reader % 2, half, reader // 2, pair * 16:(pair + 1) * 16] = (
                    jnp.concatenate([results[0][at], results[1][at]], axis=0)
                )
        half_copy(half).start()
    for half in range(2):
        half_copy(half).wait_recv()
        for n in range(NZ):
            target = z_at(n)
            leaving[half, target] = (outgoing[core, half, target] + from_half[half, target]).astype(BF)
            if n < NZ - 1:
                out_copy(half, n).start()
            else:
                own_copy(half).start()
    for step in range(1, NX):
        for half in range(2):
            row_copy(half, step).wait_send()

    @pl.when(t > 0)
    def _():
        for target in range(NX):
            first_copy(target).wait_send()

    for half in range(2):
        half_copy(half).wait_send()
    series_copy.wait()
    for half in range(2):
        sent_out(half).wait_recv()

    for half in range(2):
        sent_out(half).wait_send()
        own_copy(half).wait()


def finish(series_in, arrived, series, stacked):
    series[...] = series_in[...]
    for half in range(2):
        total = arrived[half, 0].astype(F32)
        for source in range(1, NZ):
            total = total + arrived[half, source].astype(F32)
        for i in range(NACC // 2):
            stacked[half * (NACC // 2) + i] = total[i * TRIALS:(i + 1) * TRIALS].astype(BF)


def on_device(filterbank, channel_mask, delays, readers, stretch):
    hbm = pl.BlockSpec(memory_space=pltpu.HBM)
    vmem = pl.BlockSpec(memory_space=pltpu.VMEM)
    dma = pltpu.SemaphoreType.DMA
    results = pl.pallas_call(
        kernel,
        out_shape=(
            jax.ShapeDtypeStruct((TRIALS, SHARD), BF),
            jax.ShapeDtypeStruct((2, NZ, NACC * TRIALS // 2, BLK), BF),
        ),
        in_specs=[hbm] * 5,
        out_specs=(hbm, hbm),
        scratch_shapes=[
            pltpu.VMEM((TRIALS, SHARD), BF),
            pltpu.VMEM(filterbank.shape, BF),
            pltpu.SMEM((OWN,), jnp.int32),
            pltpu.SMEM((NACC,), F32),
            pltpu.SMEM((OWN, N_CHAN * TRIALS), jnp.int32),
            pltpu.VMEM((NACC, 1, ROWS), jnp.int32),
            pltpu.VMEM((NX, NACC, 1, ROWS), jnp.int32),
            pltpu.VMEM((PAIRS, ROWS, BLK), F32),
            pltpu.VMEM((PAIRS, ROWS, BLK), F32),
            pltpu.VMEM((PAIRS, ROWS, BLK), F32),
            pltpu.VMEM((PAIRS, ROWS, BLK), BF),
            pltpu.VMEM((PAIRS, ROWS, BLK), BF),
            pltpu.VMEM((PAIRS, BLK), F32),
            pltpu.VMEM((PAIRS, BLK), F32),
            pltpu.VMEM((PAIRS, BLK), F32),
            pltpu.VMEM((PAIRS + 1, 1, BLK), F32),
            pltpu.VMEM((PAIRS, 1, BLK), F32),
            pltpu.VMEM((ROWS, BLK), F32),
            pltpu.VMEM((2, N_CHAN - 1, HALF * GROUP, BLK), BF),
            pltpu.VMEM((2, N_CHAN, HALF * GROUP, BLK), BF),
            pltpu.VMEM((2 * BLK, STEPS * BLK), BF),
            pltpu.VMEM((OWN, REACH, BLK), F32),
            pltpu.VMEM((NACC, 2 * BLK, BLK), BF),
            pltpu.VMEM((TRIALS * ROWS, BLK), F32),
            pltpu.VMEM((2, BLK, BLK), BF),
            pltpu.VMEM((16, BLK), BF),
            pltpu.VMEM((NX, 2, BLK, BLK), BF),
            pltpu.VMEM((NX, 16, BLK), BF),
            pltpu.VMEM((TRIALS, NX, ROWS + 8, BLK), F32),
            pltpu.VMEM((NACC, 2, TRIALS * NQ, BLK), F32),
            pltpu.VMEM((2, 2, NZ, NACC * TRIALS // 2, BLK), F32),
            pltpu.VMEM((2, NZ, NACC * TRIALS // 2, BLK), F32),
            pltpu.VMEM((2, NZ, NACC * TRIALS // 2, BLK), BF),
            dma((4,)),
            dma,
            dma((PAIRS,)),
            dma((NX,)),
            dma((NX,)),
            dma,
            dma,
            dma((2,)),
            dma,
            dma,
            dma((2, N_CHAN)),
            dma((2, N_CHAN)),
            dma((NX,)),
            dma((NX,)),
            dma((2, NX)),
            dma((2, NX)),
            dma((NX,)),
            dma((NX,)),
            dma((2,)),
            dma((2,)),
            dma((2,)),
            dma((2,)),
            dma((2,)),
        ],
        compiler_params=pltpu.CompilerParams(
            collective_id=0, has_side_effects=True, vmem_limit_bytes=60 * 2**20
        ),
        name="dedisperse",
    )(
        filterbank, channel_mask, delays.T, jnp.transpose(readers, (1, 2, 0)), stretch
    )
    return pl.pallas_call(
        finish,
        out_shape=(
            jax.ShapeDtypeStruct((TRIALS, SHARD), BF),
            jax.ShapeDtypeStruct((NACC, TRIALS, BLK), BF),
        ),
        in_specs=[vmem] * 2,
        out_specs=(vmem, vmem),
        compiler_params=pltpu.CompilerParams(vmem_limit_bytes=60 * 2**20),
        name="results",
    )(*results)


def solution(mesh):
    return jax.shard_map(
        on_device,
        mesh=mesh,
        in_specs=(
            P(("chan", "tm"), None),
            P(("chan", "tm")),
            P(None, "chan"),
            P("tm", None, None),
            P(),
        ),
        out_specs=(P("chan", "tm"), P(None, "chan", "tm")),
        check_vma=False,
    )
```

```python
import math

import jax
import jax.numpy as jnp
from jax import lax
from jax.experimental import pallas as pl
from jax.experimental.pallas import tpu as pltpu
from jax.sharding import PartitionSpec as P

MESH = pl.DeviceIdType.MESH
BF, F32 = jnp.bfloat16, jnp.float32

BLK = 128
N_TM = 64
N_CHAN = 4
SHARD = 4096
ROWS = SHARD // BLK
PAIRS = N_TM // 2
OWN = 16
TRIALS = 8
HALF = TRIALS // 2
NX = 4
NQ = 16
NZ = 8
FAR_X = (2, 1, 3, 0)
FAR_Z = (4, 3, 5, 2, 6, 1, 7, 0)
NACC = 8
GROUP = 32
LANE_GROUPS = BLK // GROUP
STACKS = OWN // LANE_GROUPS
STEPS = 4
REACH = GROUP * (STEPS + 1)
CHUNK = 4
START_OFFSET = 4.0
TAPER_HALF = 8.0


def remote(src, dst, send_sem, recv_sem, tm, chan):
    return pltpu.make_async_remote_copy(
        src_ref=src,
        dst_ref=dst,
        send_sem=send_sem,
        recv_sem=recv_sem,
        device_id=(tm, chan),
        device_id_type=MESH,
    )


def sinc_tables(stretch, table):
    row = lax.broadcasted_iota(jnp.int32, (8, BLK), 0)
    col = lax.broadcasted_iota(jnp.int32, (8, BLK), 1).astype(F32)
    factor = jnp.zeros((8, BLK), F32)
    for a in range(NACC):
        factor = jnp.where(row == a, stretch[a], factor)
    centres = START_OFFSET + col * factor
    whole = jnp.round(centres)
    odd = whole - 2.0 * jnp.floor(whole * 0.5)
    waves = (2.0 * odd - 1.0) * jnp.sin(math.pi * (centres - whole)) / math.pi
    angle = (math.pi / TAPER_HALF) * (centres - 16.0 * jnp.floor(centres / 16.0))
    cosines, sines = 0.5 * jnp.cos(angle), 0.5 * jnp.sin(angle)
    sign = (1 - 2 * (row % 2)).astype(F32)
    turns = [(math.pi / TAPER_HALF) * (row + 8 * half).astype(F32) for half in range(2)]
    turns = [(jnp.cos(angle), jnp.sin(angle)) for angle in turns]
    for a in range(NACC):
        centre, wave, cos_p, sin_p = (
            jnp.broadcast_to(part[a:a + 1], (8, BLK)) for part in (centres, waves, cosines, sines)
        )
        wave = sign * wave
        tapers = [0.5 + cos_j * cos_p + sin_j * sin_p for cos_j, sin_j in turns]
        pieces = []
        for group in range(2 * BLK // 8):
            x = (row + 8 * group).astype(F32) - centre
            sinc = jnp.where(x == 0.0, 1.0, wave / jnp.where(x == 0.0, 1.0, x))
            pieces.append(jnp.where(jnp.abs(x) < TAPER_HALF, sinc * tapers[group % 2], 0.0))
        table[a] = jnp.concatenate(pieces, axis=0).astype(BF)


def turn(blocks):
    lane_group = lax.broadcasted_iota(jnp.int32, (ROWS, BLK), 1) // GROUP
    stacked = []
    for g in range(LANE_GROUPS):
        merged = blocks[0]
        for i in range(LANE_GROUPS):
            shift = (i - g) * GROUP % BLK
            moved = pltpu.roll(blocks[i], shift, 1) if shift else blocks[i]
            merged = moved if i == 0 else jnp.where(lane_group == i, moved, merged)
        stacked.append(merged)
    return jnp.concatenate(stacked, axis=0).T


def turn_back(rows):
    lane_group = lax.broadcasted_iota(jnp.int32, (ROWS, BLK), 1) // GROUP
    flipped = rows.T
    out = []
    for i in range(LANE_GROUPS):
        merged = None
        for g in range(LANE_GROUPS):
            piece = flipped[g * ROWS:(g + 1) * ROWS]
            shift = (g - i) * GROUP % BLK
            moved = pltpu.roll(piece, shift, 1) if shift else piece
            merged = moved if g == 0 else jnp.where(lane_group == g, moved, merged)
        out.append(merged)
    return out


def lane_steps():
    shape = (2 * BLK, STEPS * BLK)
    row = lax.broadcasted_iota(jnp.int32, shape, 0)
    col = lax.broadcasted_iota(jnp.int32, shape, 1)
    group = (col % BLK) // GROUP + col // BLK + 1
    block = col % GROUP + group // LANE_GROUPS
    group = group % LANE_GROUPS
    inside = (row == group * GROUP + block) & (block < ROWS)
    beyond = (row // GROUP == LANE_GROUPS + group) & (block == ROWS)
    return jnp.where(inside | beyond, 1.0, 0.0).astype(BF)


def kernel(
    fb, mask_in, delays_in, readers_in, stretch_in,
    series_out, arrived,
    series, fb_v, mask, stretch, delays, readers_v, readers_all,
    for_core, own_sum, from_core, staged, parts,
    for_first, own_first, from_first, next_row, next_parts, halo_f,
    trials_out, trials_in, steps, reach,
    table, turned, rows, first, gathered, first_all, tall, grouped,
    outgoing, from_half, leaving,
    small_sem, result_sem, load_sem, core_send, core_recv, part_send, part_recv,
    first_core_sem, next_send, next_recv, trial_send, trial_recv,
    reader_send, reader_recv, row_send, row_recv, first_send, first_recv,
    half_send, half_recv, out_send, out_recv, own_sem,
):
    t, c = lax.axis_index("tm"), lax.axis_index("chan")
    core, me = lax.rem(t, 2), t // 2
    other = t + 1 - 2 * core
    x, q = t // NQ, lax.rem(t, NQ)
    z = q // 2

    small = [
        pltpu.make_async_copy(source, target, small_sem.at[i])
        for i, (source, target) in enumerate(
            ((mask_in, mask), (delays_in, delays), (readers_in, readers_v), (stretch_in, stretch))
        )
    ]
    for copy in small:
        copy.start()

    turn_side = 1 - 2 * core

    def chip_at(chunk, i, parity):
        if isinstance(chunk, int):
            half, dx = chunk // 4, FAR_X[chunk % 4]
        else:
            half, g = chunk // 4, lax.rem(chunk, 4)
            dx = 2 - g + 3 * (g // 2) - 2 * (g // 3)
        dz = FAR_Z[i] + half * (FAR_Z[CHUNK + i] - FAR_Z[i])
        side = 1 - 2 * parity
        return NZ * lax.rem(x + NX + side * dx, NX) + lax.rem(z + NZ + side * dz, NZ)

    def load(n):
        at = pl.ds(pl.multiple_of(n * 2 * SHARD, 2 * SHARD), 2 * SHARD)
        return pltpu.make_async_copy(fb.at[:, at], fb_v.at[:, at], load_sem.at[n])

    def start_load(n, carry):
        load(n).start()
        return carry

    def greet_plane(n, carry):
        greet(lax.rem(t + n, N_TM), c)
        return carry

    def greet(tm, chan):
        pl.semaphore_signal(barrier, inc=1, device_id=(tm, chan), device_id_type=MESH)

    barrier = pltpu.get_barrier_semaphore()
    lax.fori_loop(0, 8, start_load, 0)
    lax.fori_loop(24, 48, greet_plane, 0)
    lax.fori_loop(8, PAIRS, start_load, 0)
    lax.fori_loop(1, 24, greet_plane, 0)
    lax.fori_loop(48, N_TM, greet_plane, 0)
    for step in range(1, N_CHAN):
        greet(t, lax.rem(c + step, N_CHAN))

    for copy in small:
        copy.wait()
    sublane = lax.broadcasted_iota(jnp.int32, (8, BLK), 0)
    weights = []
    for half in range(2):
        value = jnp.zeros((8, BLK), F32)
        for i in range(8):
            value = jnp.where(sublane == i, mask[8 * half + i].astype(F32), value)
        weights.append(value)

    def block_sum(at):
        block = fb_v[:, pl.ds(at, BLK)].astype(F32)
        return block[:8] * weights[0] + block[8:] * weights[1]

    def merge(blocks):
        step = 1
        while len(blocks) > 1:
            even = (sublane // step) % 2 == 0
            blocks = [
                jnp.where(even, a, b) + pltpu.roll(jnp.where(even, b, a), 8 - step, 0)
                for a, b in zip(blocks[0::2], blocks[1::2])
            ]
            step *= 2
        return blocks[0]

    def shard_sum(shard):
        base = pl.multiple_of(shard * SHARD, SHARD)
        return jnp.concatenate(
            [
                merge([block_sum(base + (8 * group + i) * BLK) for i in range(8)])
                for group in range(ROWS // 8)
            ],
            axis=0,
        )

    def to_core(row):
        at = pl.ds(pl.multiple_of(row * NZ, NZ), NZ)
        return remote(
            for_core.at[at], from_core.at[at], core_send.at[row], core_recv.at[row], other, c
        )


    def sum_chip(n, carry):
        load(n).wait()
        for_core[n] = shard_sum(2 * n + 1 - core)
        own_sum[n] = shard_sum(2 * n + core)
        for_first[n] = for_core[n, :1]
        own_first[n] = own_sum[n, :1]
        return carry

    lax.fori_loop(0, PAIRS, sum_chip, 0)
    pl.semaphore_wait(barrier, N_TM - 1 + N_CHAN - 1)

    first_to_core = remote(
        own_first, from_first, first_core_sem.at[0], first_core_sem.at[1], other, c
    )

    first_to_core.start()
    for g in range(NX):
        to_core(lax.rem(x + NX - turn_side * FAR_X[g], NX)).start()

    def reader_copy(step):
        return remote(
            readers_v, readers_all.at[x], reader_send.at[step - 1], reader_recv.at[x],
            lax.rem(x + step, NX) * NQ + q, c,
        )

    readers_all[x] = readers_v[...]

    def send_part(chunk, i):
        chip = chip_at(chunk, i, core)
        return remote(
            staged.at[chip], parts.at[me], part_send, part_recv,
            2 * chip + core, c,
        )

    def send_parts(chunk, carry):
        for i in range(CHUNK):
            chip = chip_at(chunk, i, core)
            staged[chip] = (own_sum[chip] + from_core[chip]).astype(BF)
            if i < CHUNK - 1 or isinstance(chunk, int):
                send_part(chunk, i).start()
                send_next(chunk, i).start()
            else:
                @pl.when(chunk < PAIRS // CHUNK - 1)
                def _():
                    send_part(chunk, i).start()
                    send_next(chunk, i).start()

        return carry

    def send_next(chunk, i):
        chip = chip_at(chunk, i, core)
        return remote(
            next_row.at[chip + core], next_parts.at[me], next_send, next_recv,
            2 * chip + core, c,
        )

    first_to_core.wait_recv()
    next_row[PAIRS:] = jnp.zeros((1, 1, BLK), F32)
    next_row[:PAIRS] = for_first[...] + from_first[...]

    for chunk in range(NX):
        to_core(lax.rem(x + NX + turn_side * FAR_X[chunk], NX)).wait_recv()
        send_parts(chunk, 0)
    lax.fori_loop(NX, PAIRS // CHUNK, send_parts, 0)
    for step in range(1, NX):
        reader_copy(step).start()
    parts[me] = staged[me]
    next_parts[me] = next_row[me + core]

    sinc_tables(stretch, table)
    steps[...] = lane_steps()
    halo_f[...] = jnp.zeros_like(halo_f)
    for step in range(1, NX):
        source = lax.rem(x + step, NX)
        remote(
            readers_v, readers_all.at[source], reader_send.at[0], reader_recv.at[source],
            source * NQ + q, c,
        ).wait_recv()
    names = jnp.concatenate([readers_all[source][:, 0, :] for source in range(NX)], axis=1)
    reader_row = lax.broadcasted_iota(jnp.int32, (NQ, BLK), 0) + x * NQ
    pick = jnp.concatenate(
        [(names[a:a + 1] == reader_row).astype(F32) for a in range(NACC)], axis=0
    ).astype(BF)

    others = pl.ds(0, PAIRS - 1)
    all_parts = remote(parts.at[others], parts.at[others], part_send, part_recv, other, c)
    all_nexts = remote(
        next_parts.at[others], next_parts.at[others], next_send, next_recv, other, c
    )
    all_parts.wait_recv()
    own = []
    for stack in range(STACKS):
        blocks = []
        for k in range(stack * LANE_GROUPS, (stack + 1) * LANE_GROUPS):
            blocks.append(parts[2 * k].astype(F32) + parts[2 * k + 1].astype(F32))
        own.append(turn(blocks).astype(BF))
    own = jnp.concatenate(own, axis=0)
    reach[:, :GROUP] = own.astype(F32).reshape(OWN, GROUP, BLK)

    all_nexts.wait_recv()
    for k in range(OWN):
        halo_f[k:k + 1] = next_parts[2 * k] + next_parts[2 * k + 1]
    first_blocks = halo_f[...]
    beyond = jnp.concatenate(
        [first_blocks] + [pltpu.roll(first_blocks, BLK - g * GROUP, 1) for g in range(1, LANE_GROUPS)],
        axis=0,
    ).T[:GROUP]
    lane = lax.broadcasted_iota(jnp.int32, (GROUP, BLK), 1)
    next_blocks = jnp.concatenate(
        [jnp.where(lane % GROUP == k, beyond, 0.0).astype(BF) for k in range(OWN)], axis=0
    )
    both = jnp.concatenate([own, next_blocks], axis=1)
    for pair in range(STEPS // 2):
        moved = jnp.dot(
            both, steps[:, pair * 2 * BLK:(pair + 1) * 2 * BLK], preferred_element_type=F32
        )
        for i in range(2):
            e = 2 * pair + i + 1
            reach[:, e * GROUP:(e + 1) * GROUP] = moved[:, i * BLK:(i + 1) * BLK].reshape(
                OWN, GROUP, BLK
            )

    def trials_of(chan, half):
        def one_band(k, sums):
            return tuple(
                sums[m] + reach[k, pl.ds(delays[k, chan * TRIALS + half * HALF + m], GROUP)]
                for m in range(HALF)
            )

        sums = tuple(jnp.zeros((GROUP, BLK), F32) for _ in range(HALF))
        return jnp.concatenate(lax.fori_loop(0, OWN, one_band, sums, unroll=2), axis=0)

    def chan_at(step):
        return lax.rem(c + N_CHAN + turn_side * step, N_CHAN)

    def trial_copy(half, step):
        return remote(
            trials_out.at[half, step - 1], trials_in.at[half, c],
            trial_send.at[half, step - 1], trial_recv.at[half, c], t, chan_at(step),
        )

    for half in range(2):
        for step in (2, 1, 3):
            trials_out[half, step - 1] = trials_of(chan_at(step), half).astype(BF)
            trial_copy(half, step).start()
    totals = [trials_of(c, half) for half in range(2)]
    for row in range(NX):
        to_core(row).wait_send()
    first_to_core.wait_send()
    all_parts.wait_send()
    all_nexts.wait_send()
    for step in range(1, NX):
        reader_copy(step).wait_send()

    def row_copy(half, step):
        return remote(
            rows.at[half], gathered.at[x, half], row_send.at[half, step - 1], row_recv.at[half, x],
            lax.rem(x + NX + turn_side * step, NX) * NQ + q, c,
        )

    def first_copy(half, target):
        return remote(
            first.at[half], first_all.at[half, (t - 1) // NQ], first_send.at[half, target],
            first_recv.at[half, (t - 1) // NQ], target * NQ + lax.rem(t - 1, NQ), c,
        )

    backs = []
    for half in range(2):
        total = totals[half]
        for step in (1, 3, 2):
            source = chan_at(step)
            remote(
                trials_out.at[half, 0], trials_in.at[half, source],
                trial_send.at[half, 0], trial_recv.at[half, source], t, source,
            ).wait_recv()
            total = total + trials_in[half, source].astype(F32)
        back = turn_back(total)
        backs += back
        first[half] = jnp.concatenate(
            [block[:1] for block in back] + [jnp.zeros((16 - HALF, BLK), F32)], axis=0
        ).astype(BF)

        @pl.when(t > 0)
        def _():
            for target in range(NX):
                first_copy(half, target).start()

        for i in range(HALF):
            rows[half, i * ROWS:(i + 1) * ROWS] = back[i].astype(BF)
        for step in (2, 1, 3):
            row_copy(half, step).start()
    gathered[x] = rows[...]
    for m in range(TRIALS):
        turned[pl.ds(m, ROWS, stride=TRIALS)] = backs[m]
    for b in range(ROWS):
        series[:, b * BLK:(b + 1) * BLK] = turned[b * TRIALS:(b + 1) * TRIALS].astype(BF)

    series_copy = pltpu.make_async_copy(series, series_out, result_sem)
    series_copy.start()

    for half in range(2):
        for step in range(1, N_CHAN):
            trial_copy(half, step).wait_send()

    def first_arrival(half, source):
        return remote(
            first.at[half], first_all.at[half, source], first_send.at[half, 0],
            first_recv.at[half, source], source * NQ + q + 1, c,
        )

    def half_copy(half):
        return remote(
            outgoing.at[1 - core, half], from_half.at[half], half_send.at[half], half_recv.at[half],
            other, c,
        )

    def z_at(n):
        return lax.rem(z + NZ + turn_side * FAR_Z[n], NZ)

    def out_copy(half, n):
        target = z_at(n)
        return remote(
            leaving.at[half, target], arrived.at[half, z],
            out_send.at[half], out_recv.at[half], x * NQ + 2 * target + core, c,
        )

    def sent_out(half):
        others = pl.ds(0, NZ - 1)
        return remote(
            leaving.at[half, others], arrived.at[half, others],
            out_send.at[half], out_recv.at[half], other, c,
        )

    def own_copy(half):
        return pltpu.make_async_copy(
            leaving.at[half, z], arrived.at[half, z], own_sem.at[half]
        )

    def send_out(half):
        half_copy(half).wait_recv()
        for n in range(NZ):
            target = z_at(n)
            leaving[half, target] = (outgoing[core, half, target] + from_half[half, target]).astype(BF)
            if n < NZ - 1:
                out_copy(half, n).start()
            else:
                own_copy(half).start()

    def group(i, upper, block):
        sums = jnp.dot(pick, block, preferred_element_type=F32)
        for a in range(NACC):
            grouped[a, upper, pl.ds(i, NQ, stride=HALF)] = sums[a * NQ:(a + 1) * NQ]

    for half in range(2):
        for step in (1, 3, 2):
            source = lax.rem(x + step, NX)
            remote(
                rows.at[half], gathered.at[source, half], row_send.at[half, 0],
                row_recv.at[half, source], source * NQ + q, c,
            ).wait_recv()
        if half == 1:
            send_out(0)
        for i in range(HALF):
            at = i * ROWS
            pieces = [gathered[source, half, at:at + ROWS] for source in range(NX)]
            group(i, 0, jnp.concatenate(pieces, axis=0))
            for source in range(NX):
                tall[i, source, :ROWS] = pieces[source].astype(F32)
        for source in range(NX):
            last_block = source * NQ + q == N_TM - 1

            @pl.when(jnp.logical_not(last_block))
            def _():
                first_arrival(half, source).wait_recv()

            @pl.when(last_block)
            def _():
                first_all[half, source] = jnp.zeros((16, BLK), BF)

            last = first_all[half, source].astype(F32)
            for i in range(HALF):
                tall[i, source, ROWS:ROWS + 1] = last[i:i + 1]
        for i in range(HALF):
            pieces = [tall[i, source, 1:1 + ROWS] for source in range(NX)]
            group(i, 1, jnp.concatenate(pieces, axis=0).astype(BF))
        for pair in range(NACC // 2):
            results = []
            for a in (2 * pair, 2 * pair + 1):
                block = jnp.concatenate([grouped[a, 0], grouped[a, 1]], axis=1).astype(BF)
                results.append(jnp.dot(block, table[a], preferred_element_type=F32))
            for reader in range(NQ):
                at = slice(reader * HALF, (reader + 1) * HALF)
                outgoing[reader % 2, half, reader // 2, pair * 8:(pair + 1) * 8] = (
                    jnp.concatenate([results[0][at], results[1][at]], axis=0)
                )
        half_copy(half).start()
    send_out(1)
    for step in range(1, NX):
        for half in range(2):
            row_copy(half, step).wait_send()

    @pl.when(t > 0)
    def _():
        for half in range(2):
            for target in range(NX):
                first_copy(half, target).wait_send()

    for half in range(2):
        half_copy(half).wait_send()
    series_copy.wait()
    for half in range(2):
        sent_out(half).wait_recv()

    for half in range(2):
        sent_out(half).wait_send()
        own_copy(half).wait()


def finish(series_in, arrived, series, stacked):
    series[...] = series_in[...]
    halves = []
    for half in range(2):
        total = arrived[half, 0].astype(F32)
        for source in range(1, NZ):
            total = total + arrived[half, source].astype(F32)
        halves.append(total)
    for a in range(NACC):
        at = slice(a * HALF, (a + 1) * HALF)
        stacked[a] = jnp.concatenate([total[at] for total in halves], axis=0).astype(BF)


def on_device(filterbank, channel_mask, delays, readers, stretch):
    hbm = pl.BlockSpec(memory_space=pltpu.HBM)
    vmem = pl.BlockSpec(memory_space=pltpu.VMEM)
    dma = pltpu.SemaphoreType.DMA
    results = pl.pallas_call(
        kernel,
        out_shape=(
            jax.ShapeDtypeStruct((TRIALS, SHARD), BF),
            jax.ShapeDtypeStruct((2, NZ, NACC * TRIALS // 2, BLK), BF),
        ),
        in_specs=[hbm] * 5,
        out_specs=(hbm, hbm),
        scratch_shapes=[
            pltpu.VMEM((TRIALS, SHARD), BF),
            pltpu.VMEM(filterbank.shape, BF),
            pltpu.SMEM((OWN,), jnp.int32),
            pltpu.SMEM((NACC,), F32),
            pltpu.SMEM((OWN, N_CHAN * TRIALS), jnp.int32),
            pltpu.VMEM((NACC, 1, ROWS), jnp.int32),
            pltpu.VMEM((NX, NACC, 1, ROWS), jnp.int32),
            pltpu.VMEM((PAIRS, ROWS, BLK), F32),
            pltpu.VMEM((PAIRS, ROWS, BLK), F32),
            pltpu.VMEM((PAIRS, ROWS, BLK), F32),
            pltpu.VMEM((PAIRS, ROWS, BLK), BF),
            pltpu.VMEM((PAIRS, ROWS, BLK), BF),
            pltpu.VMEM((PAIRS, 1, BLK), F32),
            pltpu.VMEM((PAIRS, 1, BLK), F32),
            pltpu.VMEM((PAIRS, 1, BLK), F32),
            pltpu.VMEM((PAIRS + 1, 1, BLK), F32),
            pltpu.VMEM((PAIRS, 1, BLK), F32),
            pltpu.VMEM((ROWS, BLK), F32),
            pltpu.VMEM((2, N_CHAN - 1, HALF * GROUP, BLK), BF),
            pltpu.VMEM((2, N_CHAN, HALF * GROUP, BLK), BF),
            pltpu.VMEM((2 * BLK, STEPS * BLK), BF),
            pltpu.VMEM((OWN, REACH, BLK), F32),
            pltpu.VMEM((NACC, 2 * BLK, BLK), BF),
            pltpu.VMEM((TRIALS * ROWS, BLK), F32),
            pltpu.VMEM((2, BLK, BLK), BF),
            pltpu.VMEM((2, 16, BLK), BF),
            pltpu.VMEM((NX, 2, BLK, BLK), BF),
            pltpu.VMEM((2, NX, 16, BLK), BF),
            pltpu.VMEM((HALF, NX, ROWS + 8, BLK), F32),
            pltpu.VMEM((NACC, 2, HALF * NQ, BLK), F32),
            pltpu.VMEM((2, 2, NZ, NACC * TRIALS // 2, BLK), F32),
            pltpu.VMEM((2, NZ, NACC * TRIALS // 2, BLK), F32),
            pltpu.VMEM((2, NZ, NACC * TRIALS // 2, BLK), BF),
            dma((4,)),
            dma,
            dma((PAIRS,)),
            dma((NX,)),
            dma((NX,)),
            dma,
            dma,
            dma((2,)),
            dma,
            dma,
            dma((2, N_CHAN)),
            dma((2, N_CHAN)),
            dma((NX,)),
            dma((NX,)),
            dma((2, NX)),
            dma((2, NX)),
            dma((2, NX)),
            dma((2, NX)),
            dma((2,)),
            dma((2,)),
            dma((2,)),
            dma((2,)),
            dma((2,)),
        ],
        compiler_params=pltpu.CompilerParams(
            collective_id=0, has_side_effects=True, vmem_limit_bytes=60 * 2**20
        ),
        name="dedisperse",
    )(
        filterbank, channel_mask, delays.T, jnp.transpose(readers, (1, 2, 0)), stretch
    )
    return pl.pallas_call(
        finish,
        out_shape=(
            jax.ShapeDtypeStruct((TRIALS, SHARD), BF),
            jax.ShapeDtypeStruct((NACC, TRIALS, BLK), BF),
        ),
        in_specs=[vmem] * 2,
        out_specs=(vmem, vmem),
        compiler_params=pltpu.CompilerParams(vmem_limit_bytes=60 * 2**20),
        name="results",
    )(*results)


def solution(mesh):
    return jax.shard_map(
        on_device,
        mesh=mesh,
        in_specs=(
            P(("chan", "tm"), None),
            P(("chan", "tm")),
            P(None, "chan"),
            P("tm", None, None),
            P(),
        ),
        out_specs=(P("chan", "tm"), P(None, "chan", "tm")),
        check_vma=False,
    )
```

```python
import math

import jax
import jax.numpy as jnp
from jax import lax
from jax.experimental import pallas as pl
from jax.experimental.pallas import tpu as pltpu
from jax.sharding import PartitionSpec as P

MESH = pl.DeviceIdType.MESH
BF, F32 = jnp.bfloat16, jnp.float32

BLK = 128
N_TM = 64
N_CHAN = 4
SHARD = 4096
ROWS = SHARD // BLK
PAIRS = N_TM // 2
OWN = 16
TRIALS = 8
HALF = TRIALS // 2
NX = 4
NQ = 16
NZ = 8
FAR_X = (2, 1, 3, 0)
OWN_CHIP = (7, 3)
FAR_Z = (4, 3, 5, 2, 6, 1, 7, 0)
NACC = 8
GROUP = 32
LANE_GROUPS = BLK // GROUP
STACKS = OWN // LANE_GROUPS
STEPS = 4
REACH = GROUP * (STEPS + 1)
CHUNK = 4
START_OFFSET = 4.0
TAPER_HALF = 8.0


def remote(src, dst, send_sem, recv_sem, tm, chan):
    return pltpu.make_async_remote_copy(
        src_ref=src,
        dst_ref=dst,
        send_sem=send_sem,
        recv_sem=recv_sem,
        device_id=(tm, chan),
        device_id_type=MESH,
    )


def sinc_tables(stretch, table):
    row = lax.broadcasted_iota(jnp.int32, (8, BLK), 0)
    col = lax.broadcasted_iota(jnp.int32, (8, BLK), 1).astype(F32)
    factor = jnp.zeros((8, BLK), F32)
    for a in range(NACC):
        factor = jnp.where(row == a, stretch[a], factor)
    centres = START_OFFSET + col * factor
    whole = jnp.round(centres)
    odd = whole - 2.0 * jnp.floor(whole * 0.5)
    waves = (2.0 * odd - 1.0) * jnp.sin(math.pi * (centres - whole)) / math.pi
    angle = (math.pi / TAPER_HALF) * (centres - 16.0 * jnp.floor(centres / 16.0))
    cosines, sines = 0.5 * jnp.cos(angle), 0.5 * jnp.sin(angle)
    sign = (1 - 2 * (row % 2)).astype(F32)
    turns = [(math.pi / TAPER_HALF) * (row + 8 * half).astype(F32) for half in range(2)]
    turns = [(jnp.cos(angle), jnp.sin(angle)) for angle in turns]
    for a in range(NACC):
        centre, wave, cos_p, sin_p = (
            jnp.broadcast_to(part[a:a + 1], (8, BLK)) for part in (centres, waves, cosines, sines)
        )
        wave = sign * wave
        tapers = [0.5 + cos_j * cos_p + sin_j * sin_p for cos_j, sin_j in turns]
        pieces = []
        for group in range(2 * BLK // 8):
            x = (row + 8 * group).astype(F32) - centre
            sinc = jnp.where(x == 0.0, 1.0, wave / jnp.where(x == 0.0, 1.0, x))
            pieces.append(jnp.where(jnp.abs(x) < TAPER_HALF, sinc * tapers[group % 2], 0.0))
        table[a] = jnp.concatenate(pieces, axis=0).astype(BF)


def turn(blocks):
    lane_group = lax.broadcasted_iota(jnp.int32, (ROWS, BLK), 1) // GROUP
    stacked = []
    for g in range(LANE_GROUPS):
        merged = blocks[0]
        for i in range(LANE_GROUPS):
            shift = (i - g) * GROUP % BLK
            moved = pltpu.roll(blocks[i], shift, 1) if shift else blocks[i]
            merged = moved if i == 0 else jnp.where(lane_group == i, moved, merged)
        stacked.append(merged)
    return jnp.concatenate(stacked, axis=0).T


def turn_back(rows):
    lane_group = lax.broadcasted_iota(jnp.int32, (ROWS, BLK), 1) // GROUP
    flipped = rows.T
    out = []
    for i in range(LANE_GROUPS):
        merged = None
        for g in range(LANE_GROUPS):
            piece = flipped[g * ROWS:(g + 1) * ROWS]
            shift = (g - i) * GROUP % BLK
            moved = pltpu.roll(piece, shift, 1) if shift else piece
            merged = moved if g == 0 else jnp.where(lane_group == g, moved, merged)
        out.append(merged)
    return out


def lane_steps():
    shape = (2 * BLK, STEPS * BLK)
    row = lax.broadcasted_iota(jnp.int32, shape, 0)
    col = lax.broadcasted_iota(jnp.int32, shape, 1)
    group = (col % BLK) // GROUP + col // BLK + 1
    block = col % GROUP + group // LANE_GROUPS
    group = group % LANE_GROUPS
    inside = (row == group * GROUP + block) & (block < ROWS)
    beyond = (row // GROUP == LANE_GROUPS + group) & (block == ROWS)
    return jnp.where(inside | beyond, 1.0, 0.0).astype(BF)


def kernel(
    fb, mask_in, delays_in, readers_in, stretch_in,
    series_out, arrived,
    series, fb_v, mask, stretch, delays, readers_v, readers_all,
    for_core, own_sum, from_core, staged, parts,
    for_first, own_first, from_first, next_row, next_parts, halo_f,
    trials_out, trials_in, steps, reach,
    table, turned, rows, first, gathered, first_all, tall, grouped,
    outgoing, from_half, leaving,
    small_sem, result_sem, load_sem, core_send, core_recv, part_send, part_recv,
    first_core_sem, next_send, next_recv, trial_send, trial_recv,
    reader_send, reader_recv, row_send, row_recv, first_send, first_recv,
    half_send, half_recv, out_send, out_recv, own_sem,
):
    t, c = lax.axis_index("tm"), lax.axis_index("chan")
    core, me = lax.rem(t, 2), t // 2
    other = t + 1 - 2 * core
    x, q = t // NQ, lax.rem(t, NQ)
    z = q // 2

    small = [
        pltpu.make_async_copy(source, target, small_sem.at[i])
        for i, (source, target) in enumerate(
            ((mask_in, mask), (delays_in, delays), (readers_in, readers_v), (stretch_in, stretch))
        )
    ]
    for copy in small:
        copy.start()

    turn_side = 1 - 2 * core

    def chip_at(chunk, i, parity):
        dx, dz = FAR_X[chunk % NX], FAR_Z[chunk // NX * CHUNK + i]
        side = 1 - 2 * parity
        return NZ * lax.rem(x + NX + side * dx, NX) + lax.rem(z + NZ + side * dz, NZ)

    def load(n):
        at = pl.ds(pl.multiple_of(n * 2 * SHARD, 2 * SHARD), 2 * SHARD)
        return pltpu.make_async_copy(fb.at[:, at], fb_v.at[:, at], load_sem.at[n])

    def start_load(n, carry):
        load(n).start()
        return carry

    def row_at(g):
        return lax.rem(x + FAR_X[g], NX)

    def start_row(g):
        lax.fori_loop(row_at(g) * NZ, row_at(g) * NZ + NZ, start_load, 0)

    def greet_plane(n, carry):
        greet(lax.rem(t + n, N_TM), c)
        return carry

    def greet(tm, chan):
        pl.semaphore_signal(barrier, inc=1, device_id=(tm, chan), device_id_type=MESH)

    barrier = pltpu.get_barrier_semaphore()
    lax.fori_loop(24, 32, greet_plane, 0)
    start_row(0)
    lax.fori_loop(32, 48, greet_plane, 0)
    for g in range(1, NX):
        start_row(g)
    lax.fori_loop(1, 24, greet_plane, 0)
    lax.fori_loop(48, N_TM, greet_plane, 0)
    for step in range(1, N_CHAN):
        greet(t, lax.rem(c + step, N_CHAN))

    for copy in small:
        copy.wait()
    sublane = lax.broadcasted_iota(jnp.int32, (8, BLK), 0)
    weights = []
    for half in range(2):
        value = jnp.zeros((8, BLK), F32)
        for i in range(8):
            value = jnp.where(sublane == i, mask[8 * half + i].astype(F32), value)
        weights.append(value)

    def block_sum(at):
        block = fb_v[:, pl.ds(at, BLK)].astype(F32)
        return block[:8] * weights[0] + block[8:] * weights[1]

    def merge(blocks):
        step = 1
        while len(blocks) > 1:
            even = (sublane // step) % 2 == 0
            blocks = [
                jnp.where(even, a, b) + pltpu.roll(jnp.where(even, b, a), 8 - step, 0)
                for a, b in zip(blocks[0::2], blocks[1::2])
            ]
            step *= 2
        return blocks[0]

    def shard_sum(shard):
        base = pl.multiple_of(shard * SHARD, SHARD)
        return jnp.concatenate(
            [
                merge([block_sum(base + (8 * group + i) * BLK) for i in range(8)])
                for group in range(ROWS // 8)
            ],
            axis=0,
        )

    def to_core(row):
        at = pl.ds(pl.multiple_of(row * NZ, NZ), NZ)
        return remote(
            for_core.at[at], from_core.at[at], core_send.at[row], core_recv.at[row], other, c
        )


    def sum_chip(n, carry):
        load(n).wait()
        for_core[n] = shard_sum(2 * n + 1 - core)
        own_sum[n] = shard_sum(2 * n + core)
        for_first[n] = for_core[n, :1]
        own_first[n] = own_sum[n, :1]
        return carry

    def sum_row(g):
        lax.fori_loop(row_at(g) * NZ, row_at(g) * NZ + NZ, sum_chip, 0)

    for g in range(NX - 1):
        sum_row(g)
    pl.semaphore_wait(barrier, N_TM - 1 + N_CHAN - 1)

    first_to_core = remote(
        own_first, from_first, first_core_sem.at[0], first_core_sem.at[1], other, c
    )

    for g in range(NX - 1):
        to_core(lax.rem(x + NX - turn_side * FAR_X[g], NX)).start()
    sum_row(NX - 1)
    first_to_core.start()
    to_core(x).start()

    def reader_copy(step):
        return remote(
            readers_v, readers_all.at[x], reader_send.at[step - 1], reader_recv.at[x],
            lax.rem(x + step, NX) * NQ + q, c,
        )

    readers_all[x] = readers_v[...]

    def send_part(chunk, i):
        chip = chip_at(chunk, i, core)
        return remote(
            staged.at[chip], parts.at[me], part_send, part_recv,
            2 * chip + core, c,
        )

    def send_parts(chunk):
        for i in range(CHUNK):
            chip = chip_at(chunk, i, core)
            staged[chip] = (own_sum[chip] + from_core[chip]).astype(BF)
            if (chunk, i) != OWN_CHIP:
                send_part(chunk, i).start()
                if chunk:
                    send_next(chunk, i).start()

    def send_next(chunk, i):
        chip = chip_at(chunk, i, core)
        return remote(
            next_row.at[chip + core], next_parts.at[me], next_send, next_recv,
            2 * chip + core, c,
        )

    for chunk in range(PAIRS // CHUNK):
        if chunk < NX:
            to_core(lax.rem(x + NX + turn_side * FAR_X[chunk], NX)).wait_recv()
        send_parts(chunk)
        if chunk == 0:
            first_to_core.wait_recv()
            next_row[PAIRS:] = jnp.zeros((1, 1, BLK), F32)
            next_row[:PAIRS] = for_first[...] + from_first[...]
            for i in range(CHUNK):
                send_next(chunk, i).start()
    for step in range(1, NX):
        reader_copy(step).start()
    parts[me] = staged[me]
    next_parts[me] = next_row[me + core]

    sinc_tables(stretch, table)
    steps[...] = lane_steps()
    halo_f[...] = jnp.zeros_like(halo_f)
    for step in range(1, NX):
        source = lax.rem(x + step, NX)
        remote(
            readers_v, readers_all.at[source], reader_send.at[0], reader_recv.at[source],
            source * NQ + q, c,
        ).wait_recv()
    names = jnp.concatenate([readers_all[source][:, 0, :] for source in range(NX)], axis=1)
    reader_row = lax.broadcasted_iota(jnp.int32, (NQ, BLK), 0) + x * NQ
    pick = jnp.concatenate(
        [(names[a:a + 1] == reader_row).astype(F32) for a in range(NACC)], axis=0
    ).astype(BF)

    others = pl.ds(0, PAIRS - 1)
    all_parts = remote(parts.at[others], parts.at[others], part_send, part_recv, other, c)
    all_nexts = remote(
        next_parts.at[others], next_parts.at[others], next_send, next_recv, other, c
    )
    all_parts.wait_recv()
    own = []
    for stack in range(STACKS):
        blocks = []
        for k in range(stack * LANE_GROUPS, (stack + 1) * LANE_GROUPS):
            blocks.append(parts[2 * k].astype(F32) + parts[2 * k + 1].astype(F32))
        own.append(turn(blocks).astype(BF))
    own = jnp.concatenate(own, axis=0)
    reach[:, :GROUP] = own.astype(F32).reshape(OWN, GROUP, BLK)

    all_nexts.wait_recv()
    for k in range(OWN):
        halo_f[k:k + 1] = next_parts[2 * k] + next_parts[2 * k + 1]
    first_blocks = halo_f[...]
    beyond = jnp.concatenate(
        [first_blocks] + [pltpu.roll(first_blocks, BLK - g * GROUP, 1) for g in range(1, LANE_GROUPS)],
        axis=0,
    ).T[:GROUP]
    lane = lax.broadcasted_iota(jnp.int32, (GROUP, BLK), 1)
    next_blocks = jnp.concatenate(
        [jnp.where(lane % GROUP == k, beyond, 0.0).astype(BF) for k in range(OWN)], axis=0
    )
    both = jnp.concatenate([own, next_blocks], axis=1)
    for pair in range(STEPS // 2):
        moved = jnp.dot(
            both, steps[:, pair * 2 * BLK:(pair + 1) * 2 * BLK], preferred_element_type=F32
        )
        for i in range(2):
            e = 2 * pair + i + 1
            reach[:, e * GROUP:(e + 1) * GROUP] = moved[:, i * BLK:(i + 1) * BLK].reshape(
                OWN, GROUP, BLK
            )

    def trials_of(chan, half):
        def one_band(k, sums):
            return tuple(
                sums[m] + reach[k, pl.ds(delays[k, chan * TRIALS + half * HALF + m], GROUP)]
                for m in range(HALF)
            )

        sums = tuple(jnp.zeros((GROUP, BLK), F32) for _ in range(HALF))
        return jnp.concatenate(lax.fori_loop(0, OWN, one_band, sums, unroll=2), axis=0)

    def chan_at(step):
        return lax.rem(c + N_CHAN + turn_side * step, N_CHAN)

    def trial_copy(half, step):
        return remote(
            trials_out.at[half, step - 1], trials_in.at[half, c],
            trial_send.at[half, step - 1], trial_recv.at[half, c], t, chan_at(step),
        )

    for half in range(2):
        for step in (2, 1, 3):
            trials_out[half, step - 1] = trials_of(chan_at(step), half).astype(BF)
            trial_copy(half, step).start()
    totals = [trials_of(c, half) for half in range(2)]
    for row in range(NX):
        to_core(row).wait_send()
    first_to_core.wait_send()
    all_parts.wait_send()
    all_nexts.wait_send()
    for step in range(1, NX):
        reader_copy(step).wait_send()

    def row_copy(half, step):
        return remote(
            rows.at[half], gathered.at[x, half], row_send.at[half, step - 1], row_recv.at[half, x],
            lax.rem(x + NX + turn_side * step, NX) * NQ + q, c,
        )

    def first_copy(half, target):
        return remote(
            first.at[half], first_all.at[half, (t - 1) // NQ], first_send.at[half, target],
            first_recv.at[half, (t - 1) // NQ], target * NQ + lax.rem(t - 1, NQ), c,
        )

    backs = []
    for half in range(2):
        total = totals[half]
        for step in (1, 3, 2):
            source = chan_at(step)
            remote(
                trials_out.at[half, 0], trials_in.at[half, source],
                trial_send.at[half, 0], trial_recv.at[half, source], t, source,
            ).wait_recv()
            total = total + trials_in[half, source].astype(F32)
        back = turn_back(total)
        backs += back
        first[half] = jnp.concatenate(
            [block[:1] for block in back] + [jnp.zeros((16 - HALF, BLK), F32)], axis=0
        ).astype(BF)

        @pl.when(t > 0)
        def _():
            for target in range(NX):
                first_copy(half, target).start()

        for i in range(HALF):
            rows[half, i * ROWS:(i + 1) * ROWS] = back[i].astype(BF)
        for step in (2, 1, 3):
            row_copy(half, step).start()
    gathered[x] = rows[...]
    for m in range(TRIALS):
        turned[pl.ds(m, ROWS, stride=TRIALS)] = backs[m]
    for b in range(ROWS):
        series[:, b * BLK:(b + 1) * BLK] = turned[b * TRIALS:(b + 1) * TRIALS].astype(BF)

    series_copy = pltpu.make_async_copy(series, series_out, result_sem)
    series_copy.start()

    for half in range(2):
        for step in range(1, N_CHAN):
            trial_copy(half, step).wait_send()

    def first_arrival(half, source):
        return remote(
            first.at[half], first_all.at[half, source], first_send.at[half, 0],
            first_recv.at[half, source], source * NQ + q + 1, c,
        )

    def half_copy(half):
        return remote(
            outgoing.at[1 - core, half], from_half.at[half], half_send.at[half], half_recv.at[half],
            other, c,
        )

    def z_at(n):
        return lax.rem(z + NZ + turn_side * FAR_Z[n], NZ)

    def out_copy(half, n):
        target = z_at(n)
        return remote(
            leaving.at[half, target], arrived.at[half, z],
            out_send.at[half], out_recv.at[half], x * NQ + 2 * target + core, c,
        )

    def sent_out(half):
        others = pl.ds(0, NZ - 1)
        return remote(
            leaving.at[half, others], arrived.at[half, others],
            out_send.at[half], out_recv.at[half], other, c,
        )

    def own_copy(half):
        return pltpu.make_async_copy(
            leaving.at[half, z], arrived.at[half, z], own_sem.at[half]
        )

    def send_out(half):
        half_copy(half).wait_recv()
        for n in range(NZ):
            target = z_at(n)
            leaving[half, target] = (outgoing[core, half, target] + from_half[half, target]).astype(BF)
            if n < NZ - 1:
                out_copy(half, n).start()
            else:
                own_copy(half).start()

    def group(i, upper, block):
        sums = jnp.dot(pick, block, preferred_element_type=F32)
        for a in range(NACC):
            grouped[a, upper, pl.ds(i, NQ, stride=HALF)] = sums[a * NQ:(a + 1) * NQ]

    for half in range(2):
        for step in (1, 3, 2):
            source = lax.rem(x + step, NX)
            remote(
                rows.at[half], gathered.at[source, half], row_send.at[half, 0],
                row_recv.at[half, source], source * NQ + q, c,
            ).wait_recv()
        if half == 1:
            send_out(0)
        for i in range(HALF):
            at = i * ROWS
            pieces = [gathered[source, half, at:at + ROWS] for source in range(NX)]
            group(i, 0, jnp.concatenate(pieces, axis=0))
            for source in range(NX):
                tall[i, source, :ROWS] = pieces[source].astype(F32)
        for source in range(NX):
            last_block = source * NQ + q == N_TM - 1

            @pl.when(jnp.logical_not(last_block))
            def _():
                first_arrival(half, source).wait_recv()

            @pl.when(last_block)
            def _():
                first_all[half, source] = jnp.zeros((16, BLK), BF)

            last = first_all[half, source].astype(F32)
            for i in range(HALF):
                tall[i, source, ROWS:ROWS + 1] = last[i:i + 1]
        for i in range(HALF):
            pieces = [tall[i, source, 1:1 + ROWS] for source in range(NX)]
            group(i, 1, jnp.concatenate(pieces, axis=0).astype(BF))
        for pair in range(NACC // 2):
            results = []
            for a in (2 * pair, 2 * pair + 1):
                block = jnp.concatenate([grouped[a, 0], grouped[a, 1]], axis=1).astype(BF)
                results.append(jnp.dot(block, table[a], preferred_element_type=F32))
            for reader in range(NQ):
                at = slice(reader * HALF, (reader + 1) * HALF)
                outgoing[reader % 2, half, reader // 2, pair * 8:(pair + 1) * 8] = (
                    jnp.concatenate([results[0][at], results[1][at]], axis=0)
                )
        half_copy(half).start()
    send_out(1)
    for step in range(1, NX):
        for half in range(2):
            row_copy(half, step).wait_send()

    @pl.when(t > 0)
    def _():
        for half in range(2):
            for target in range(NX):
                first_copy(half, target).wait_send()

    for half in range(2):
        half_copy(half).wait_send()
    series_copy.wait()
    for half in range(2):
        sent_out(half).wait_recv()

    for half in range(2):
        sent_out(half).wait_send()
        own_copy(half).wait()


def finish(series_in, arrived, series, stacked):
    series[...] = series_in[...]
    halves = []
    for half in range(2):
        total = arrived[half, 0].astype(F32)
        for source in range(1, NZ):
            total = total + arrived[half, source].astype(F32)
        halves.append(total)
    for a in range(NACC):
        at = slice(a * HALF, (a + 1) * HALF)
        stacked[a] = jnp.concatenate([total[at] for total in halves], axis=0).astype(BF)


def on_device(filterbank, channel_mask, delays, readers, stretch):
    hbm = pl.BlockSpec(memory_space=pltpu.HBM)
    vmem = pl.BlockSpec(memory_space=pltpu.VMEM)
    dma = pltpu.SemaphoreType.DMA
    results = pl.pallas_call(
        kernel,
        out_shape=(
            jax.ShapeDtypeStruct((TRIALS, SHARD), BF),
            jax.ShapeDtypeStruct((2, NZ, NACC * TRIALS // 2, BLK), BF),
        ),
        in_specs=[hbm] * 5,
        out_specs=(hbm, hbm),
        scratch_shapes=[
            pltpu.VMEM((TRIALS, SHARD), BF),
            pltpu.VMEM(filterbank.shape, BF),
            pltpu.SMEM((OWN,), jnp.int32),
            pltpu.SMEM((NACC,), F32),
            pltpu.SMEM((OWN, N_CHAN * TRIALS), jnp.int32),
            pltpu.VMEM((NACC, 1, ROWS), jnp.int32),
            pltpu.VMEM((NX, NACC, 1, ROWS), jnp.int32),
            pltpu.VMEM((PAIRS, ROWS, BLK), F32),
            pltpu.VMEM((PAIRS, ROWS, BLK), F32),
            pltpu.VMEM((PAIRS, ROWS, BLK), F32),
            pltpu.VMEM((PAIRS, ROWS, BLK), BF),
            pltpu.VMEM((PAIRS, ROWS, BLK), BF),
            pltpu.VMEM((PAIRS, 1, BLK), F32),
            pltpu.VMEM((PAIRS, 1, BLK), F32),
            pltpu.VMEM((PAIRS, 1, BLK), F32),
            pltpu.VMEM((PAIRS + 1, 1, BLK), F32),
            pltpu.VMEM((PAIRS, 1, BLK), F32),
            pltpu.VMEM((ROWS, BLK), F32),
            pltpu.VMEM((2, N_CHAN - 1, HALF * GROUP, BLK), BF),
            pltpu.VMEM((2, N_CHAN, HALF * GROUP, BLK), BF),
            pltpu.VMEM((2 * BLK, STEPS * BLK), BF),
            pltpu.VMEM((OWN, REACH, BLK), F32),
            pltpu.VMEM((NACC, 2 * BLK, BLK), BF),
            pltpu.VMEM((TRIALS * ROWS, BLK), F32),
            pltpu.VMEM((2, BLK, BLK), BF),
            pltpu.VMEM((2, 16, BLK), BF),
            pltpu.VMEM((NX, 2, BLK, BLK), BF),
            pltpu.VMEM((2, NX, 16, BLK), BF),
            pltpu.VMEM((HALF, NX, ROWS + 8, BLK), F32),
            pltpu.VMEM((NACC, 2, HALF * NQ, BLK), F32),
            pltpu.VMEM((2, 2, NZ, NACC * TRIALS // 2, BLK), F32),
            pltpu.VMEM((2, NZ, NACC * TRIALS // 2, BLK), F32),
            pltpu.VMEM((2, NZ, NACC * TRIALS // 2, BLK), BF),
            dma((4,)),
            dma,
            dma((PAIRS,)),
            dma((NX,)),
            dma((NX,)),
            dma,
            dma,
            dma((2,)),
            dma,
            dma,
            dma((2, N_CHAN)),
            dma((2, N_CHAN)),
            dma((NX,)),
            dma((NX,)),
            dma((2, NX)),
            dma((2, NX)),
            dma((2, NX)),
            dma((2, NX)),
            dma((2,)),
            dma((2,)),
            dma((2,)),
            dma((2,)),
            dma((2,)),
        ],
        compiler_params=pltpu.CompilerParams(
            collective_id=0, has_side_effects=True, vmem_limit_bytes=60 * 2**20
        ),
        name="dedisperse",
    )(
        filterbank, channel_mask, delays.T, jnp.transpose(readers, (1, 2, 0)), stretch
    )
    return pl.pallas_call(
        finish,
        out_shape=(
            jax.ShapeDtypeStruct((TRIALS, SHARD), BF),
            jax.ShapeDtypeStruct((NACC, TRIALS, BLK), BF),
        ),
        in_specs=[vmem] * 2,
        out_specs=(vmem, vmem),
        compiler_params=pltpu.CompilerParams(vmem_limit_bytes=60 * 2**20),
        name="results",
    )(*results)


def solution(mesh):
    return jax.shard_map(
        on_device,
        mesh=mesh,
        in_specs=(
            P(("chan", "tm"), None),
            P(("chan", "tm")),
            P(None, "chan"),
            P("tm", None, None),
            P(),
        ),
        out_specs=(P("chan", "tm"), P(None, "chan", "tm")),
        check_vma=False,
    )
```

```python
import math

import jax
import jax.numpy as jnp
from jax import lax
from jax.experimental import pallas as pl
from jax.experimental.pallas import tpu as pltpu
from jax.sharding import PartitionSpec as P

MESH = pl.DeviceIdType.MESH
BF, F32 = jnp.bfloat16, jnp.float32

BLK = 128
N_TM = 64
N_CHAN = 4
SHARD = 4096
ROWS = SHARD // BLK
PAIRS = N_TM // 2
OWN = 16
TRIALS = 8
HALF = TRIALS // 2
NX = 4
NQ = 16
NZ = 8
FAR_X = (2, 1, 3, 0)
FAR_Z = (4, 3, 5, 2, 6, 1, 7, 0)
NACC = 8
GROUP = 32
LANE_GROUPS = BLK // GROUP
STACKS = OWN // LANE_GROUPS
STEPS = 4
REACH = GROUP * (STEPS + 1)
CHUNK = 4
START_OFFSET = 4.0
TAPER_HALF = 8.0


def remote(src, dst, send_sem, recv_sem, tm, chan):
    return pltpu.make_async_remote_copy(
        src_ref=src,
        dst_ref=dst,
        send_sem=send_sem,
        recv_sem=recv_sem,
        device_id=(tm, chan),
        device_id_type=MESH,
    )


def sinc_tables(stretch, table):
    row = lax.broadcasted_iota(jnp.int32, (8, BLK), 0)
    col = lax.broadcasted_iota(jnp.int32, (8, BLK), 1).astype(F32)
    factor = jnp.zeros((8, BLK), F32)
    for a in range(NACC):
        factor = jnp.where(row == a, stretch[a], factor)
    centres = START_OFFSET + col * factor
    whole = jnp.round(centres)
    odd = whole - 2.0 * jnp.floor(whole * 0.5)
    waves = (2.0 * odd - 1.0) * jnp.sin(math.pi * (centres - whole)) / math.pi
    angle = (math.pi / TAPER_HALF) * (centres - 16.0 * jnp.floor(centres / 16.0))
    cosines, sines = 0.5 * jnp.cos(angle), 0.5 * jnp.sin(angle)
    sign = (1 - 2 * (row % 2)).astype(F32)
    turns = [(math.pi / TAPER_HALF) * (row + 8 * half).astype(F32) for half in range(2)]
    turns = [(jnp.cos(angle), jnp.sin(angle)) for angle in turns]
    for a in range(NACC):
        centre, wave, cos_p, sin_p = (
            jnp.broadcast_to(part[a:a + 1], (8, BLK)) for part in (centres, waves, cosines, sines)
        )
        wave = sign * wave
        tapers = [0.5 + cos_j * cos_p + sin_j * sin_p for cos_j, sin_j in turns]
        pieces = []
        for group in range(2 * BLK // 8):
            x = (row + 8 * group).astype(F32) - centre
            sinc = jnp.where(x == 0.0, 1.0, wave / jnp.where(x == 0.0, 1.0, x))
            pieces.append(jnp.where(jnp.abs(x) < TAPER_HALF, sinc * tapers[group % 2], 0.0))
        table[a] = jnp.concatenate(pieces, axis=0).astype(BF)


def turn(blocks):
    lane_group = lax.broadcasted_iota(jnp.int32, (ROWS, BLK), 1) // GROUP
    stacked = []
    for g in range(LANE_GROUPS):
        merged = blocks[0]
        for i in range(LANE_GROUPS):
            shift = (i - g) * GROUP % BLK
            moved = pltpu.roll(blocks[i], shift, 1) if shift else blocks[i]
            merged = moved if i == 0 else jnp.where(lane_group == i, moved, merged)
        stacked.append(merged)
    return jnp.concatenate(stacked, axis=0).T


def turn_back(rows):
    lane_group = lax.broadcasted_iota(jnp.int32, (ROWS, BLK), 1) // GROUP
    flipped = rows.T
    out = []
    for i in range(LANE_GROUPS):
        merged = None
        for g in range(LANE_GROUPS):
            piece = flipped[g * ROWS:(g + 1) * ROWS]
            shift = (g - i) * GROUP % BLK
            moved = pltpu.roll(piece, shift, 1) if shift else piece
            merged = moved if g == 0 else jnp.where(lane_group == g, moved, merged)
        out.append(merged)
    return out


def lane_steps():
    shape = (2 * BLK, STEPS * BLK)
    row = lax.broadcasted_iota(jnp.int32, shape, 0)
    col = lax.broadcasted_iota(jnp.int32, shape, 1)
    group = (col % BLK) // GROUP + col // BLK + 1
    block = col % GROUP + group // LANE_GROUPS
    group = group % LANE_GROUPS
    inside = (row == group * GROUP + block) & (block < ROWS)
    beyond = (row // GROUP == LANE_GROUPS + group) & (block == ROWS)
    return jnp.where(inside | beyond, 1.0, 0.0).astype(BF)


def kernel(
    fb, mask_in, delays_in, readers_in, stretch_in,
    series_out, arrived,
    series, fb_v, mask, stretch, delays, readers_v, readers_all,
    for_core, own_sum, from_core, staged, parts,
    for_first, own_first, from_first, next_row, next_parts, halo_f,
    trials_out, trials_in, steps, reach,
    table, turned, rows, first, gathered, first_all, tall, grouped,
    outgoing, from_half, leaving,
    small_sem, result_sem, load_sem, core_send, core_recv, part_send, part_recv,
    first_core_sem, next_send, next_recv, trial_send, trial_recv,
    reader_send, reader_recv, row_send, row_recv, first_send, first_recv,
    half_send, half_recv, out_send, out_recv, own_sem,
):
    t, c = lax.axis_index("tm"), lax.axis_index("chan")
    core, me = lax.rem(t, 2), t // 2
    other = t + 1 - 2 * core
    x, q = t // NQ, lax.rem(t, NQ)
    z = q // 2

    small = [
        pltpu.make_async_copy(source, target, small_sem.at[i])
        for i, (source, target) in enumerate(
            ((mask_in, mask), (delays_in, delays), (readers_in, readers_v), (stretch_in, stretch))
        )
    ]
    for copy in small:
        copy.start()

    turn_side = 1 - 2 * core

    def chip_at(chunk, i, parity):
        if isinstance(chunk, int):
            half, dx = chunk // 4, FAR_X[chunk % 4]
        else:
            half, g = chunk // 4, lax.rem(chunk, 4)
            dx = 2 - g + 3 * (g // 2) - 2 * (g // 3)
        dz = FAR_Z[i] + half * (FAR_Z[CHUNK + i] - FAR_Z[i])
        side = 1 - 2 * parity
        return NZ * lax.rem(x + NX + side * dx, NX) + lax.rem(z + NZ + side * dz, NZ)

    def load(n):
        at = pl.ds(pl.multiple_of(n * 2 * SHARD, 2 * SHARD), 2 * SHARD)
        return pltpu.make_async_copy(fb.at[:, at], fb_v.at[:, at], load_sem.at[n])

    def start_load(n, carry):
        load(n).start()
        return carry

    def greet_plane(n, carry):
        greet(lax.rem(t + n, N_TM), c)
        return carry

    def greet(tm, chan):
        pl.semaphore_signal(barrier, inc=1, device_id=(tm, chan), device_id_type=MESH)

    barrier = pltpu.get_barrier_semaphore()
    lax.fori_loop(0, 8, start_load, 0)
    lax.fori_loop(24, 48, greet_plane, 0)
    lax.fori_loop(8, PAIRS, start_load, 0)
    lax.fori_loop(1, 24, greet_plane, 0)
    lax.fori_loop(48, N_TM, greet_plane, 0)
    for step in range(1, N_CHAN):
        greet(t, lax.rem(c + step, N_CHAN))

    for copy in small:
        copy.wait()
    sublane = lax.broadcasted_iota(jnp.int32, (8, BLK), 0)
    weights = []
    for half in range(2):
        value = jnp.zeros((8, BLK), F32)
        for i in range(8):
            value = jnp.where(sublane == i, mask[8 * half + i].astype(F32), value)
        weights.append(value)

    def block_sum(at):
        block = fb_v[:, pl.ds(at, BLK)].astype(F32)
        return block[:8] * weights[0] + block[8:] * weights[1]

    def merge(blocks):
        step = 1
        while len(blocks) > 1:
            even = (sublane // step) % 2 == 0
            blocks = [
                jnp.where(even, a, b) + pltpu.roll(jnp.where(even, b, a), 8 - step, 0)
                for a, b in zip(blocks[0::2], blocks[1::2])
            ]
            step *= 2
        return blocks[0]

    def shard_sum(shard):
        base = pl.multiple_of(shard * SHARD, SHARD)
        return jnp.concatenate(
            [
                merge([block_sum(base + (8 * group + i) * BLK) for i in range(8)])
                for group in range(ROWS // 8)
            ],
            axis=0,
        )

    def to_core(row):
        at = pl.ds(pl.multiple_of(row * NZ, NZ), NZ)
        return remote(
            for_core.at[at], from_core.at[at], core_send.at[row], core_recv.at[row], other, c
        )


    def sum_chip(n, carry):
        load(n).wait()
        for_core[n] = shard_sum(2 * n + 1 - core)
        own_sum[n] = shard_sum(2 * n + core)
        for_first[n] = for_core[n, :1]
        own_first[n] = own_sum[n, :1]
        return carry

    lax.fori_loop(0, PAIRS, sum_chip, 0)
    pl.semaphore_wait(barrier, N_TM - 1 + N_CHAN - 1)

    first_to_core = remote(
        own_first, from_first, first_core_sem.at[0], first_core_sem.at[1], other, c
    )

    first_to_core.start()
    for g in range(NX):
        to_core(lax.rem(x + NX - turn_side * FAR_X[g], NX)).start()

    def reader_copy(step):
        return remote(
            readers_v, readers_all.at[x], reader_send.at[step - 1], reader_recv.at[x],
            lax.rem(x + step, NX) * NQ + q, c,
        )

    readers_all[x] = readers_v[...]

    def send_part(chunk, i):
        chip = chip_at(chunk, i, core)
        return remote(
            staged.at[chip], parts.at[me], part_send, part_recv,
            2 * chip + core, c,
        )

    def send_parts(chunk, carry):
        for i in range(CHUNK):
            chip = chip_at(chunk, i, core)
            staged[chip] = (own_sum[chip] + from_core[chip]).astype(BF)
            if i < CHUNK - 1 or isinstance(chunk, int):
                send_part(chunk, i).start()
                send_next(chunk, i).start()
            else:
                @pl.when(chunk < PAIRS // CHUNK - 1)
                def _():
                    send_part(chunk, i).start()
                    send_next(chunk, i).start()

        return carry

    def send_next(chunk, i):
        chip = chip_at(chunk, i, core)
        return remote(
            next_row.at[chip + core], next_parts.at[me], next_send, next_recv,
            2 * chip + core, c,
        )

    first_to_core.wait_recv()
    next_row[PAIRS:] = jnp.zeros((1, 1, BLK), F32)
    next_row[:PAIRS] = for_first[...] + from_first[...]

    for chunk in range(NX):
        to_core(lax.rem(x + NX + turn_side * FAR_X[chunk], NX)).wait_recv()
        send_parts(chunk, 0)
    lax.fori_loop(NX, PAIRS // CHUNK, send_parts, 0)
    for step in range(1, NX):
        reader_copy(step).start()
    parts[me] = staged[me]
    next_parts[me] = next_row[me + core]

    sinc_tables(stretch, table)
    steps[...] = lane_steps()
    halo_f[...] = jnp.zeros_like(halo_f)
    for step in range(1, NX):
        source = lax.rem(x + step, NX)
        remote(
            readers_v, readers_all.at[source], reader_send.at[0], reader_recv.at[source],
            source * NQ + q, c,
        ).wait_recv()
    names = jnp.concatenate([readers_all[source][:, 0, :] for source in range(NX)], axis=1)
    reader_row = lax.broadcasted_iota(jnp.int32, (NQ, BLK), 0) + x * NQ
    pick = jnp.concatenate(
        [(names[a:a + 1] == reader_row).astype(F32) for a in range(NACC)], axis=0
    ).astype(BF)

    others = pl.ds(0, PAIRS - 1)
    all_parts = remote(parts.at[others], parts.at[others], part_send, part_recv, other, c)
    all_nexts = remote(
        next_parts.at[others], next_parts.at[others], next_send, next_recv, other, c
    )
    all_parts.wait_recv()
    own = []
    for stack in range(STACKS):
        blocks = []
        for k in range(stack * LANE_GROUPS, (stack + 1) * LANE_GROUPS):
            blocks.append(parts[2 * k].astype(F32) + parts[2 * k + 1].astype(F32))
        own.append(turn(blocks).astype(BF))
    own = jnp.concatenate(own, axis=0)
    reach[:, :GROUP] = own.astype(F32).reshape(OWN, GROUP, BLK)

    all_nexts.wait_recv()
    for k in range(OWN):
        halo_f[k:k + 1] = next_parts[2 * k] + next_parts[2 * k + 1]
    first_blocks = halo_f[...]
    beyond = jnp.concatenate(
        [first_blocks] + [pltpu.roll(first_blocks, BLK - g * GROUP, 1) for g in range(1, LANE_GROUPS)],
        axis=0,
    ).T[:GROUP]
    lane = lax.broadcasted_iota(jnp.int32, (GROUP, BLK), 1)
    next_blocks = jnp.concatenate(
        [jnp.where(lane % GROUP == k, beyond, 0.0).astype(BF) for k in range(OWN)], axis=0
    )
    both = jnp.concatenate([own, next_blocks], axis=1)
    for pair in range(STEPS // 2):
        moved = jnp.dot(
            both, steps[:, pair * 2 * BLK:(pair + 1) * 2 * BLK], preferred_element_type=F32
        )
        for i in range(2):
            e = 2 * pair + i + 1
            reach[:, e * GROUP:(e + 1) * GROUP] = moved[:, i * BLK:(i + 1) * BLK].reshape(
                OWN, GROUP, BLK
            )

    def trials_of(chan, half):
        def one_band(k, sums):
            return tuple(
                sums[m] + reach[k, pl.ds(delays[k, chan * TRIALS + half * HALF + m], GROUP)]
                for m in range(HALF)
            )

        sums = tuple(jnp.zeros((GROUP, BLK), F32) for _ in range(HALF))
        return jnp.concatenate(lax.fori_loop(0, OWN, one_band, sums, unroll=2), axis=0)

    def chan_at(step):
        return lax.rem(c + N_CHAN + turn_side * step, N_CHAN)

    def trial_copy(half, step):
        return remote(
            trials_out.at[half, step - 1], trials_in.at[half, c],
            trial_send.at[half, step - 1], trial_recv.at[half, c], t, chan_at(step),
        )

    for half in range(2):
        for step in (2, 1, 3):
            trials_out[half, step - 1] = trials_of(chan_at(step), half).astype(BF)
            trial_copy(half, step).start()
    totals = [trials_of(c, half) for half in range(2)]
    for row in range(NX):
        to_core(row).wait_send()
    first_to_core.wait_send()
    all_parts.wait_send()
    all_nexts.wait_send()
    for step in range(1, NX):
        reader_copy(step).wait_send()

    def row_copy(half, step):
        return remote(
            rows.at[half], gathered.at[x, half], row_send.at[half, step - 1], row_recv.at[half, x],
            lax.rem(x + NX + turn_side * step, NX) * NQ + q, c,
        )

    def first_copy(half, target):
        return remote(
            first.at[half], first_all.at[half, (t - 1) // NQ], first_send.at[half, target],
            first_recv.at[half, (t - 1) // NQ], target * NQ + lax.rem(t - 1, NQ), c,
        )

    backs = []
    for half in range(2):
        total = totals[half]
        for step in (1, 3, 2):
            source = chan_at(step)
            remote(
                trials_out.at[half, 0], trials_in.at[half, source],
                trial_send.at[half, 0], trial_recv.at[half, source], t, source,
            ).wait_recv()
            total = total + trials_in[half, source].astype(F32)
        back = turn_back(total)
        backs += back
        first[half] = jnp.concatenate(
            [block[:1] for block in back] + [jnp.zeros((16 - HALF, BLK), F32)], axis=0
        ).astype(BF)

        def send_first():
            @pl.when(t > 0)
            def _():
                for target in range(NX):
                    first_copy(half, target).start()

        if half == 1:
            send_first()
        for i in range(HALF):
            rows[half, i * ROWS:(i + 1) * ROWS] = back[i].astype(BF)
        for step in (2, 1, 3):
            row_copy(half, step).start()
        if half == 0:
            send_first()
    gathered[x] = rows[...]
    for m in range(TRIALS):
        turned[pl.ds(m, ROWS, stride=TRIALS)] = backs[m]
    for b in range(ROWS):
        series[:, b * BLK:(b + 1) * BLK] = turned[b * TRIALS:(b + 1) * TRIALS].astype(BF)

    series_copy = pltpu.make_async_copy(series, series_out, result_sem)
    series_copy.start()

    for half in range(2):
        for step in range(1, N_CHAN):
            trial_copy(half, step).wait_send()

    def first_arrival(half, source):
        return remote(
            first.at[half], first_all.at[half, source], first_send.at[half, 0],
            first_recv.at[half, source], source * NQ + q + 1, c,
        )

    def half_copy(half):
        return remote(
            outgoing.at[1 - core, half], from_half.at[half], half_send.at[half], half_recv.at[half],
            other, c,
        )

    def z_at(n):
        return lax.rem(z + NZ + turn_side * FAR_Z[n], NZ)

    def out_copy(half, n):
        target = z_at(n)
        return remote(
            leaving.at[half, target], arrived.at[half, z],
            out_send.at[half], out_recv.at[half], x * NQ + 2 * target + core, c,
        )

    def sent_out(half):
        others = pl.ds(0, NZ - 1)
        return remote(
            leaving.at[half, others], arrived.at[half, others],
            out_send.at[half], out_recv.at[half], other, c,
        )

    def own_copy(half):
        return pltpu.make_async_copy(
            leaving.at[half, z], arrived.at[half, z], own_sem.at[half]
        )

    def send_out(half):
        half_copy(half).wait_recv()
        for n in range(NZ):
            target = z_at(n)
            leaving[half, target] = (outgoing[core, half, target] + from_half[half, target]).astype(BF)
            if n < NZ - 1:
                out_copy(half, n).start()
            else:
                own_copy(half).start()

    def group(i, upper, block):
        sums = jnp.dot(pick, block, preferred_element_type=F32)
        for a in range(NACC):
            grouped[a, upper, pl.ds(i, NQ, stride=HALF)] = sums[a * NQ:(a + 1) * NQ]

    for half in range(2):
        for step in (1, 3, 2):
            source = lax.rem(x + step, NX)
            remote(
                rows.at[half], gathered.at[source, half], row_send.at[half, 0],
                row_recv.at[half, source], source * NQ + q, c,
            ).wait_recv()
        if half == 1:
            send_out(0)
        for i in range(HALF):
            at = i * ROWS
            pieces = [gathered[source, half, at:at + ROWS] for source in range(NX)]
            group(i, 0, jnp.concatenate(pieces, axis=0))
            for source in range(NX):
                tall[i, source, :ROWS] = pieces[source].astype(F32)
        for source in range(NX):
            last_block = source * NQ + q == N_TM - 1

            @pl.when(jnp.logical_not(last_block))
            def _():
                first_arrival(half, source).wait_recv()

            @pl.when(last_block)
            def _():
                first_all[half, source] = jnp.zeros((16, BLK), BF)

            last = first_all[half, source].astype(F32)
            for i in range(HALF):
                tall[i, source, ROWS:ROWS + 1] = last[i:i + 1]
        for i in range(HALF):
            pieces = [tall[i, source, 1:1 + ROWS] for source in range(NX)]
            group(i, 1, jnp.concatenate(pieces, axis=0).astype(BF))
        for pair in range(NACC // 2):
            results = []
            for a in (2 * pair, 2 * pair + 1):
                block = jnp.concatenate([grouped[a, 0], grouped[a, 1]], axis=1).astype(BF)
                results.append(jnp.dot(block, table[a], preferred_element_type=F32))
            for reader in range(NQ):
                at = slice(reader * HALF, (reader + 1) * HALF)
                outgoing[reader % 2, half, reader // 2, pair * 8:(pair + 1) * 8] = (
                    jnp.concatenate([results[0][at], results[1][at]], axis=0)
                )
        half_copy(half).start()
    send_out(1)
    for step in range(1, NX):
        for half in range(2):
            row_copy(half, step).wait_send()

    @pl.when(t > 0)
    def _():
        for half in range(2):
            for target in range(NX):
                first_copy(half, target).wait_send()

    for half in range(2):
        half_copy(half).wait_send()
    series_copy.wait()
    for half in range(2):
        sent_out(half).wait_recv()

    for half in range(2):
        sent_out(half).wait_send()
        own_copy(half).wait()


def finish(series_in, arrived, series, stacked):
    series[...] = series_in[...]
    halves = []
    for half in range(2):
        total = arrived[half, 0].astype(F32)
        for source in range(1, NZ):
            total = total + arrived[half, source].astype(F32)
        halves.append(total)
    for a in range(NACC):
        at = slice(a * HALF, (a + 1) * HALF)
        stacked[a] = jnp.concatenate([total[at] for total in halves], axis=0).astype(BF)


def on_device(filterbank, channel_mask, delays, readers, stretch):
    hbm = pl.BlockSpec(memory_space=pltpu.HBM)
    vmem = pl.BlockSpec(memory_space=pltpu.VMEM)
    dma = pltpu.SemaphoreType.DMA
    results = pl.pallas_call(
        kernel,
        out_shape=(
            jax.ShapeDtypeStruct((TRIALS, SHARD), BF),
            jax.ShapeDtypeStruct((2, NZ, NACC * TRIALS // 2, BLK), BF),
        ),
        in_specs=[hbm] * 5,
        out_specs=(hbm, hbm),
        scratch_shapes=[
            pltpu.VMEM((TRIALS, SHARD), BF),
            pltpu.VMEM(filterbank.shape, BF),
            pltpu.SMEM((OWN,), jnp.int32),
            pltpu.SMEM((NACC,), F32),
            pltpu.SMEM((OWN, N_CHAN * TRIALS), jnp.int32),
            pltpu.VMEM((NACC, 1, ROWS), jnp.int32),
            pltpu.VMEM((NX, NACC, 1, ROWS), jnp.int32),
            pltpu.VMEM((PAIRS, ROWS, BLK), F32),
            pltpu.VMEM((PAIRS, ROWS, BLK), F32),
            pltpu.VMEM((PAIRS, ROWS, BLK), F32),
            pltpu.VMEM((PAIRS, ROWS, BLK), BF),
            pltpu.VMEM((PAIRS, ROWS, BLK), BF),
            pltpu.VMEM((PAIRS, 1, BLK), F32),
            pltpu.VMEM((PAIRS, 1, BLK), F32),
            pltpu.VMEM((PAIRS, 1, BLK), F32),
            pltpu.VMEM((PAIRS + 1, 1, BLK), F32),
            pltpu.VMEM((PAIRS, 1, BLK), F32),
            pltpu.VMEM((ROWS, BLK), F32),
            pltpu.VMEM((2, N_CHAN - 1, HALF * GROUP, BLK), BF),
            pltpu.VMEM((2, N_CHAN, HALF * GROUP, BLK), BF),
            pltpu.VMEM((2 * BLK, STEPS * BLK), BF),
            pltpu.VMEM((OWN, REACH, BLK), F32),
            pltpu.VMEM((NACC, 2 * BLK, BLK), BF),
            pltpu.VMEM((TRIALS * ROWS, BLK), F32),
            pltpu.VMEM((2, BLK, BLK), BF),
            pltpu.VMEM((2, 16, BLK), BF),
            pltpu.VMEM((NX, 2, BLK, BLK), BF),
            pltpu.VMEM((2, NX, 16, BLK), BF),
            pltpu.VMEM((HALF, NX, ROWS + 8, BLK), F32),
            pltpu.VMEM((NACC, 2, HALF * NQ, BLK), F32),
            pltpu.VMEM((2, 2, NZ, NACC * TRIALS // 2, BLK), F32),
            pltpu.VMEM((2, NZ, NACC * TRIALS // 2, BLK), F32),
            pltpu.VMEM((2, NZ, NACC * TRIALS // 2, BLK), BF),
            dma((4,)),
            dma,
            dma((PAIRS,)),
            dma((NX,)),
            dma((NX,)),
            dma,
            dma,
            dma((2,)),
            dma,
            dma,
            dma((2, N_CHAN)),
            dma((2, N_CHAN)),
            dma((NX,)),
            dma((NX,)),
            dma((2, NX)),
            dma((2, NX)),
            dma((2, NX)),
            dma((2, NX)),
            dma((2,)),
            dma((2,)),
            dma((2,)),
            dma((2,)),
            dma((2,)),
        ],
        compiler_params=pltpu.CompilerParams(
            collective_id=0, has_side_effects=True, vmem_limit_bytes=60 * 2**20
        ),
        name="dedisperse",
    )(
        filterbank, channel_mask, delays.T, jnp.transpose(readers, (1, 2, 0)), stretch
    )
    return pl.pallas_call(
        finish,
        out_shape=(
            jax.ShapeDtypeStruct((TRIALS, SHARD), BF),
            jax.ShapeDtypeStruct((NACC, TRIALS, BLK), BF),
        ),
        in_specs=[vmem] * 2,
        out_specs=(vmem, vmem),
        compiler_params=pltpu.CompilerParams(vmem_limit_bytes=60 * 2**20),
        name="results",
    )(*results)


def solution(mesh):
    return jax.shard_map(
        on_device,
        mesh=mesh,
        in_specs=(
            P(("chan", "tm"), None),
            P(("chan", "tm")),
            P(None, "chan"),
            P("tm", None, None),
            P(),
        ),
        out_specs=(P("chan", "tm"), P(None, "chan", "tm")),
        check_vma=False,
    )
```
